32 devices in a mesh: dp: 16 (over z, y, x), tensor: 2 (over core).
Axes of the slice: x: 2, y: 2, z: 4, core: 2. Of those that a mesh axis runs over, the one named last changes fastest.
Arguments:
- inputs: bfloat16 [16384, 1024], P(('dp', 'tensor')), may hold values from -6 to 6
- segments: int32 [16384], P('dp'), may hold values from 0 to 16383, as said below
- cotangent: bfloat16 [16384, 1024], P(('dp', 'tensor')), may hold values from -6 to 6
- norm_gain: bfloat16 [1024], P(('dp', 'tensor')), may hold values from 0.5 to 1.5
- mix_in: bfloat16 [1024, 24, 128], P('dp', 'tensor'), may hold values from -0.1875 to 0.1875
- step_in: bfloat16 [1024, 24], P('dp', 'tensor'), may hold values from -0.1875 to 0.1875
- state_in: bfloat16 [1024, 256], P(('dp', 'tensor')), may hold values from -0.1875 to 0.1875
- conv_inner: bfloat16 [4, 1536], P(None, ('dp', 'tensor')), may hold values from -3 to 3
- conv_inner_bias: bfloat16 [1536], P(('dp', 'tensor')), may hold values from -1.5 to 1.5
- conv_state: bfloat16 [4, 256], P(None, ('dp', 'tensor')), may hold values from -3 to 3
- conv_state_bias: bfloat16 [256], P(('dp', 'tensor')), may hold values from -1.5 to 1.5
- decay_log: float32 [24], P('tensor'), may hold values from 0 to 2.7
- step_bias: float32 [24], P('tensor'), may hold values from -6 to -2
- skip_gain: float32 [24], P('tensor'), may hold values from 0.5 to 1.5
- mixer_gain: bfloat16 [1536], P(('dp', 'tensor')), may hold values from 0.5 to 1.5
- attn_in: bfloat16 [1024, 2, 384], P('dp', 'tensor'), may hold values from -0.1875 to 0.1875
- mixer_out: bfloat16 [24, 64, 1024], P('tensor', None, 'dp'), may hold values from -0.15625 to 0.15625
- attn_out: bfloat16 [2, 256, 1024], P('tensor', None, 'dp'), may hold values from -3 to 3
- ffn_gain: bfloat16 [1024], P(('dp', 'tensor')), may hold values from 0.5 to 1.5
- ffn_in: bfloat16 [1024, 2, 2048], P('dp', None, 'tensor'), may hold values from -0.1875 to 0.1875
- ffn_down: bfloat16 [2048, 1024], P('tensor', 'dp'), may hold values from -0.125 to 0.125
Outputs:
- output: bfloat16 [16384, 1024], P(('dp', 'tensor'))
- inputs_grad: float32 [16384, 1024], P(('dp', 'tensor'))
- norm_gain_grad: float32 [1024], P(('dp', 'tensor'))
- mix_in_grad: float32 [1024, 24, 128], P('dp', 'tensor')
- step_in_grad: float32 [1024, 24], P('dp', 'tensor')
- state_in_grad: float32 [1024, 256], P(('dp', 'tensor'))
- conv_inner_grad: float32 [4, 1536], P(None, ('dp', 'tensor'))
- conv_inner_bias_grad: float32 [1536], P(('dp', 'tensor'))
- conv_state_grad: float32 [4, 256], P(None, ('dp', 'tensor'))
- conv_state_bias_grad: float32 [256], P(('dp', 'tensor'))
- decay_log_grad: float32 [24], P('tensor')
- step_bias_grad: float32 [24], P('tensor')
- skip_gain_grad: float32 [24], P('tensor')
- mixer_gain_grad: float32 [1536], P(('dp', 'tensor'))
- attn_in_grad: float32 [1024, 2, 384], P('dp', 'tensor')
- mixer_out_grad: float32 [24, 64, 1024], P('tensor', None, 'dp')
- attn_out_grad: float32 [2, 256, 1024], P('tensor', None, 'dp')
- ffn_gain_grad: float32 [1024], P(('dp', 'tensor'))
- ffn_in_grad: float32 [1024, 2, 2048], P('dp', None, 'tensor')
- ffn_down_grad: float32 [2048, 1024], P('tensor', 'dp')
The draws below stay inside these ranges and needn't reach their ends.
Inputs may be any that keep to these rules, and one draw needn't show every extreme that they name: `segments`: each token's segment number is the index of its document's first token, so numbers never fall; every sequence of 1024 tokens begins a new document, the last token of all is a document of its own, and tokens 512 - 1 and 512 of a sequence lie in one document.
All inputs are finite; a program needn't handle non-finite values.
Results may differ from the reference program's by a relative error of at most 0.014.
Values may be sent and summed in bfloat16 or wider, within the bound.
A program may use at most 192 MiB of HBM per device.

```python
import jax
import jax.numpy as jnp
from jax import lax

D = 1024
MH = 24
HD = 64
STATE = 128
KCONV = 4
KVH = 2
QPK = 4
ADIM = 64
FF = 2048
NGH = 12
BLK = 256
DOC_LEN = 600
TOK_DEV = 512
SEQ = 1024
QBLK = 512
TOKENS = 16384


def draw_segments(key, part):
    key = jax.random.fold_in(key, 7)
    index = jnp.arange(TOKENS, dtype=jnp.int32)
    places = index % SEQ
    starts = jax.random.randint(key, (TOKENS,), 0, DOC_LEN) == 0
    starts = jnp.where(places == 0, True, starts)
    starts = jnp.where(places == TOK_DEV, False, starts)
    starts = jnp.where(index == TOKENS - 1, True, starts)
    return lax.cummax(jnp.where(starts, index, jnp.zeros_like(index)), axis=0)


def level_of(own_key, dims, pieces, smallest, high):
    loudness = 1.0
    for axis_at, shards_of in pieces:
        heights = jax.random.uniform(jax.random.fold_in(jax.random.fold_in(own_key, 6), axis_at), (shards_of,), jnp.float32, smallest / len(pieces), high / len(pieces))
        loudness = loudness * jnp.repeat(jnp.exp(heights), dims[axis_at] // shards_of).reshape((-1,) + (1,) * (len(dims) - 1 - axis_at))
    return loudness


def normal_values(rng, extent, spread, most, cuts=(), kind=jnp.bfloat16):
    entries = spread * jax.random.normal(rng, extent, jnp.float32)
    if cuts:
        entries = entries * level_of(rng, extent, cuts, -0.22, 0.18)
    return jnp.clip(entries, -most, most).astype(kind)


def setup_inputs(seed: int = 0) -> dict:
    splits = jax.random.split(jax.random.key(seed), 22)
    inputs = normal_values(splits[0], (TOKENS, D), 1.0, 6.0, ((0, 32),))
    segments = draw_segments(jax.random.fold_in(splits[21], 71), 0)
    cotangent = normal_values(splits[2], (TOKENS, D), 1.0, 6.0, ((0, 32),))
    norm_gain = jnp.clip(1.0 + 0.1 * jax.random.normal(splits[3], (D,), jnp.float32), 0.5, 1.5).astype(jnp.bfloat16)
    mix_in = normal_values(splits[4], (D, MH, 2 * HD), D ** -0.5, 0.1875, ((0, 16), (1, 2)))
    step_in = normal_values(splits[5], (D, MH), D ** -0.5, 0.1875, ((0, 16), (1, 2)))
    state_in = normal_values(splits[6], (D, 2 * STATE), D ** -0.5, 0.1875, ((0, 32),))
    conv_inner = normal_values(splits[7], (KCONV, MH * HD), KCONV ** -0.5, 3.0, ((1, 32),))
    conv_inner_bias = normal_values(splits[8], (MH * HD,), 0.3, 1.5, ((0, 32),))
    conv_state = normal_values(splits[9], (KCONV, 2 * STATE), KCONV ** -0.5, 3.0, ((1, 32),))
    conv_state_bias = normal_values(splits[10], (2 * STATE,), 0.3, 1.5, ((0, 32),))
    decay_log = jnp.clip(2.7 * jax.random.uniform(splits[11], (MH,), jnp.float32) ** level_of(splits[11], (MH,), ((0, 2),), -0.2, 0.2), 0.0, 2.7)
    step_bias = jnp.clip(-6.0 + 4.0 * jax.random.uniform(splits[12], (MH,), jnp.float32) ** level_of(splits[12], (MH,), ((0, 2),), -0.2, 0.2), -6.0, -2.0)
    skip_gain = jnp.clip(0.5 + 1.0 * jax.random.uniform(splits[13], (MH,), jnp.float32) ** level_of(splits[13], (MH,), ((0, 2),), -0.2, 0.2), 0.5, 1.5)
    mixer_gain = jnp.clip(1.0 + 0.1 * jax.random.normal(splits[14], (MH * HD,), jnp.float32), 0.5, 1.5).astype(jnp.bfloat16)
    attn_in = normal_values(splits[15], (D, KVH, (QPK + 2) * ADIM), D ** -0.5, 0.1875, ((0, 16), (1, 2)))
    mixer_out = normal_values(splits[16], (MH, HD, D), (MH * HD) ** -0.5, 0.15625, ((0, 2), (2, 16)))
    attn_out = normal_values(splits[17], (KVH, QPK * ADIM, D), 4 ** -0.5, 3.0, ((0, 2), (2, 16)))
    ffn_gain = jnp.clip(1.0 + 0.1 * jax.random.normal(splits[18], (D,), jnp.float32), 0.5, 1.5).astype(jnp.bfloat16)
    ffn_in = normal_values(splits[19], (D, 2, FF), D ** -0.5, 0.1875, ((0, 16), (2, 2)))
    ffn_down = normal_values(splits[20], (FF, D), FF ** -0.5, 0.125, ((0, 2), (1, 16)))
    return {"inputs": inputs, "segments": segments, "cotangent": cotangent, "norm_gain": norm_gain, "mix_in": mix_in, "step_in": step_in, "state_in": state_in, "conv_inner": conv_inner, "conv_inner_bias": conv_inner_bias, "conv_state": conv_state, "conv_state_bias": conv_state_bias, "decay_log": decay_log, "step_bias": step_bias, "skip_gain": skip_gain, "mixer_gain": mixer_gain, "attn_in": attn_in, "mixer_out": mixer_out, "attn_out": attn_out, "ffn_gain": ffn_gain, "ffn_in": ffn_in, "ffn_down": ffn_down}


HIGH = lax.Precision.HIGHEST
EPS = 1e-05
ROPE_BASE = 100000000000.0

@jax.custom_vjp
def low(v):
    return lax.optimization_barrier(v.astype(jnp.bfloat16)).astype(jnp.float32)

@jax.custom_vjp
def low_back(v):
    return v

def low_keep(v):
    return (low(v), None)

def low_pass(kept, grad):
    return (grad,)

def back_keep(v):
    return (v, None)

def back_low(kept, grad):
    return (low(grad),)
low.defvjp(low_keep, low_pass)
low_back.defvjp(back_keep, back_low)

def rms_gain(values, gain):
    return values * lax.rsqrt(lax.optimization_barrier(jnp.mean(values * values, -1, keepdims=True)) + EPS) * gain

def positions(segment):
    index = jnp.arange(segment.shape[0], dtype=jnp.int32)
    fresh = jnp.concatenate([jnp.ones((1,), dtype=bool), segment[1:] != segment[:-1]])
    starting = lax.cummax(jnp.where(fresh, index, jnp.zeros_like(index)), axis=0)
    return index - starting

def rotate(values, places, direction):
    half_dim = values.shape[-1] // 2
    freqs = ROPE_BASE ** (-2.0 * jnp.arange(half_dim, dtype=jnp.float32) / values.shape[-1])
    angles = places.astype(jnp.float32)[:, None] * freqs[None, :]
    bshape = (values.shape[0],) + (1,) * (values.ndim - 2) + (half_dim,)
    cosine = jnp.cos(angles).reshape(bshape)
    sine = direction * jnp.sin(angles).reshape(bshape)
    first_half = values[..., :half_dim]
    second_half = values[..., half_dim:]
    return jnp.concatenate([first_half * cosine - second_half * sine, second_half * cosine + first_half * sine], -1)

def seg_conv(values, taps, shift_bias, segment):
    n_rows = values.shape[0]
    n_taps = taps.shape[0]
    padded = jnp.pad(values, ((n_taps - 1, 0), (0, 0)))
    seg_pad = jnp.concatenate([jnp.full((n_taps - 1,), -1, dtype=jnp.int32), segment])
    result = jnp.zeros_like(values) + shift_bias[None, :]
    for offset in range(n_taps):
        same_doc = (seg_pad[offset:offset + n_rows] == segment).astype(values.dtype)
        result = result + taps[offset][None, :] * padded[offset:offset + n_rows] * same_doc[:, None]
    return result

def ssd_scan(inner, steps, decays, b_state, c_state, segment, block_len):
    n_rows, n_heads, head_dim = inner.shape
    n_blocks = n_rows // block_len
    x_blk = inner.reshape(n_blocks, block_len, n_heads, head_dim)
    dt_blk = steps.reshape(n_blocks, block_len, n_heads)
    cumul = jnp.cumsum(decays.reshape(n_blocks, block_len, n_heads), axis=1)
    b_blk = b_state.reshape(n_blocks, block_len, -1)
    c_blk = c_state.reshape(n_blocks, block_len, -1)
    seg_blk = segment.reshape(n_blocks, block_len)
    within = jnp.arange(block_len, dtype=jnp.int32)
    causal = within[:, None] >= within[None, :]
    allowed = (seg_blk[:, :, None] == seg_blk[:, None, :]) & causal[None]
    differ = cumul[:, :, None, :] - cumul[:, None, :, :]
    kernel = jnp.exp(jnp.where(allowed[..., None], differ, -1e+30))
    inner_prod = jnp.einsum('ctn,csn->cts', c_blk, b_blk, precision=HIGH)
    weights_ts = inner_prod[..., None] * kernel * dt_blk[:, None, :, :]
    y_inner = jnp.einsum('ctsh,cshp->cthp', weights_ts, x_blk, precision=HIGH)
    last_seg = seg_blk[:, -1]
    to_end = jnp.exp(cumul[:, -1:, :] - cumul) * (seg_blk == last_seg[:, None]).astype(inner.dtype)[..., None]
    local_state = jnp.einsum('csh,cshp,csn->chpn', to_end * dt_blk, x_blk, b_blk, precision=HIGH)
    prev_seg = jnp.concatenate([jnp.full((1,), -1, dtype=jnp.int32), last_seg[:-1]])
    carry_keep = jnp.exp(cumul[:, -1, :]) * (last_seg == prev_seg).astype(inner.dtype)[:, None]

    def advance(state, items):
        keep_row, fresh_state = items
        return (state * keep_row[:, None, None] + fresh_state, state)
    zero_state = jnp.zeros(local_state.shape[1:], inner.dtype)
    final_state, entering = lax.scan(advance, zero_state, (carry_keep, local_state))
    from_start = jnp.exp(cumul) * (seg_blk == prev_seg[:, None]).astype(inner.dtype)[..., None]
    y_state = jnp.einsum('ctn,chpn->cthp', c_blk, entering, precision=HIGH) * from_start[..., None]
    return (y_inner + y_state).reshape(n_rows, n_heads, head_dim)

def mamba_core(proj_zx, proj_step, proj_bc, conv_w, conv_b, conv_s, conv_sb, log_decay, bias_step, gain_skip, gain_mix, segment, block_len, group_heads):
    n_rows, n_heads, twice = proj_zx.shape
    head_dim = twice // 2
    gate_z = proj_zx[..., :head_dim]
    x_conv = jax.nn.silu(seg_conv(proj_zx[..., head_dim:].reshape(n_rows, n_heads * head_dim), conv_w, conv_b, segment))
    inner = x_conv.reshape(n_rows, n_heads, head_dim)
    bc_conv = jax.nn.silu(seg_conv(proj_bc, conv_s, conv_sb, segment))
    n_state = proj_bc.shape[1] // 2
    steps = jax.nn.softplus(proj_step + bias_step[None, :])
    decays = -steps * jnp.exp(log_decay)[None, :]
    ssm = ssd_scan(inner, steps, decays, bc_conv[:, :n_state], bc_conv[:, n_state:], segment, block_len)
    ssm = ssm + gain_skip[None, :, None] * inner
    gated = ssm * jax.nn.silu(gate_z)
    grouped = gated.reshape(n_rows, n_heads // group_heads, group_heads * head_dim)
    grouped = grouped * lax.rsqrt(lax.optimization_barrier(jnp.mean(grouped * grouped, -1, keepdims=True)) + EPS)
    return grouped.reshape(n_rows, n_heads * head_dim) * gain_mix[None, :]

def attend_block(q_blk, seg_q, place_q, keys, vals, segment, scaling):
    scores = low_back(jnp.einsum('tgqd,sgd->gqts', q_blk, keys, precision=HIGH) * scaling)
    key_places = jnp.arange(segment.shape[0], dtype=jnp.int32)
    allowed = (seg_q[:, None] == segment[None, :]) & (place_q[:, None] >= key_places[None, :])
    scores = jnp.where(allowed[None, None], scores, -1e+30)
    topmost = lax.optimization_barrier(jnp.max(scores, -1, keepdims=True))
    expo = jnp.exp(scores - topmost)
    probs = low(expo / lax.optimization_barrier(jnp.sum(expo, -1, keepdims=True)))
    return jnp.einsum('gqts,sgd->tgqd', probs, vals, precision=HIGH)

def sequence_core(items, params):
    proj_zx, proj_step, proj_bc, proj_qkv, segment = items
    conv_w, conv_b, conv_s, conv_sb, log_decay, bias_step, gain_skip, gain_mix = params
    mamba_value = mamba_core(proj_zx, proj_step, proj_bc, conv_w, conv_b, conv_s, conv_sb, log_decay, bias_step, gain_skip, gain_mix, segment, BLK, NGH)
    places = positions(segment)
    n_rows = segment.shape[0]
    q_part = proj_qkv[..., :QPK * ADIM].reshape(n_rows, KVH, QPK, ADIM)
    queries = low(rotate(q_part, places, 1.0))
    keys = low(rotate(proj_qkv[..., QPK * ADIM:(QPK + 1) * ADIM], places, 1.0))
    vals = low(proj_qkv[..., (QPK + 1) * ADIM:])
    n_q = n_rows // QBLK
    row_index = jnp.arange(n_rows, dtype=jnp.int32)

    def block_fn(block_items):
        return attend_block(block_items[0], block_items[1], block_items[2], keys, vals, segment, ADIM ** (-0.5))
    attended = lax.map(jax.checkpoint(block_fn), (queries.reshape(n_q, QBLK, KVH, QPK, ADIM), segment.reshape(n_q, QBLK), row_index.reshape(n_q, QBLK)))
    return (mamba_value, attended.reshape(n_rows, KVH, QPK * ADIM))

def layer(params, segments):
    inputs, norm_gain, mix_in, step_in, state_in, conv_inner, conv_inner_bias, conv_state, conv_state_bias, decay_log, step_bias, skip_gain, mixer_gain, attn_in, mixer_out, attn_out, ffn_gain, ffn_in, ffn_down = params
    normed = low(rms_gain(inputs, norm_gain))
    proj_zx = low_back(jnp.einsum('td,dhc->thc', normed, mix_in, precision=HIGH))
    proj_step = low_back(jnp.dot(normed, step_in, precision=HIGH))
    proj_bc = jnp.dot(normed, state_in, precision=HIGH)
    proj_qkv = low_back(jnp.einsum('td,dgc->tgc', normed, attn_in, precision=HIGH))
    n_seqs = inputs.shape[0] // SEQ
    core_params = (conv_inner, conv_inner_bias, conv_state, conv_state_bias, decay_log, step_bias, skip_gain, mixer_gain)

    def per_sequence(items):
        return sequence_core(items, core_params)
    mamba_value, attended = lax.map(jax.checkpoint(per_sequence), (proj_zx.reshape(n_seqs, SEQ, MH, 2 * HD), proj_step.reshape(n_seqs, SEQ, MH), proj_bc.reshape(n_seqs, SEQ, 2 * STATE), proj_qkv.reshape(n_seqs, SEQ, KVH, (QPK + 2) * ADIM), segments.reshape(n_seqs, SEQ)))
    mamba_value = low(mamba_value.reshape(-1, MH, HD))
    attended = low(low_back(attended.reshape(-1, KVH, QPK * ADIM)))
    mixed = jnp.einsum('thc,hcd->td', mamba_value, mixer_out, precision=HIGH) + jnp.einsum('tgc,gcd->td', attended, attn_out, precision=HIGH)
    middle = inputs + low_back(mixed)
    hidden = low(rms_gain(middle, ffn_gain))
    gate_up = low_back(jnp.einsum('td,dkf->tkf', hidden, ffn_in, precision=HIGH))
    active = low(jax.nn.silu(gate_up[:, 0]) * gate_up[:, 1])
    return middle + low_back(jnp.dot(active, ffn_down, precision=HIGH))

def reference(inputs, segments, cotangent, norm_gain, mix_in, step_in, state_in, conv_inner, conv_inner_bias, conv_state, conv_state_bias, decay_log, step_bias, skip_gain, mixer_gain, attn_in, mixer_out, attn_out, ffn_gain, ffn_in, ffn_down):
    floats = [array.astype(jnp.float32) for array in (inputs, norm_gain, mix_in, step_in, state_in, conv_inner, conv_inner_bias, conv_state, conv_state_bias, decay_log, step_bias, skip_gain, mixer_gain, attn_in, mixer_out, attn_out, ffn_gain, ffn_in, ffn_down)]

    def forward(*params):
        return layer(params, segments)
    result, pull = jax.vjp(forward, *floats)
    grads = pull(cotangent.astype(jnp.float32))
    return (result.astype(jnp.bfloat16), grads[0], grads[1], grads[2], grads[3], grads[4], grads[5], grads[6], grads[7], grads[8], grads[9], grads[10], grads[11], grads[12], grads[13], grads[14], grads[15], grads[16], grads[17], grads[18])
```

```python
import jax
import jax.numpy as jnp
from jax import lax
from jax.sharding import PartitionSpec as P

QPK = 4
ADIM = 64
NGH = 12
BLK = 256
QBLK = 512

PREC = lax.Precision.HIGH
EXACT = lax.Precision.HIGHEST
EPS = 1e-05
ROPE_BASE = 100000000000.0
F32 = jnp.float32
BF16 = jnp.bfloat16


def grid_of(size):
    if size == 16:
        return (4, 2, 2)
    factors = []
    while size % 4 == 0:
        factors.append(4)
        size //= 4
    if size > 1 or not factors:
        factors.append(size)
    return tuple(factors)


def coordinates(index, factors):
    coords = []
    for size in reversed(factors):
        coords.append(index % size)
        index = index // size
    return coords[::-1]


def pairs_of(factors, axis, keep, target):
    stride = 1
    for size in factors[axis + 1 :]:
        stride *= size
    total = 1
    for size in factors:
        total *= size
    found = []
    for index in range(total):
        place = coordinates(index, factors)[axis]
        if keep(place):
            found.append((index, index + (target(place) - place) * stride))
    return found


def gather_axis(block, factors, axis, coord):
    size = factors[axis]
    if size == 1:
        return block
    if size == 2:
        other = lax.ppermute(
            block, "dp", pairs_of(factors, axis, lambda c: True, lambda c: 1 - c)
        )
        candidates = [other, block, other]
    else:
        below, above = [], []
        upward, downward = block, block
        for step in range(1, size):
            upward = lax.ppermute(
                upward,
                "dp",
                pairs_of(factors, axis, lambda c: step - 1 <= c < size - 1, lambda c: c + 1),
            )
            downward = lax.ppermute(
                downward,
                "dp",
                pairs_of(factors, axis, lambda c: 1 <= c <= size - step, lambda c: c - 1),
            )
            below.append(upward)
            above.append(downward)
        candidates = below[::-1] + [block] + above
    return lax.dynamic_slice_in_dim(
        jnp.concatenate(candidates, axis), (size - 1 - coord) * block.shape[axis], size, axis
    )


def gather_rows(shard, factors, coords):
    n_axes = len(factors)
    half = shard.shape[0] // 2
    halves = []
    for part, order in ((0, range(1, n_axes)), (1, range(n_axes - 1, 0, -1))):
        block = shard[part * half : (part + 1) * half]
        block = block.reshape((1,) * n_axes + block.shape)
        for axis in (0, *order):
            block = gather_axis(block, factors, axis, coords[axis])
        halves.append(block)
    whole = jnp.concatenate(halves, n_axes)
    return whole.reshape(-1, shard.shape[1])


def reduce_axis(blocks, factors, axis, coord):
    size = factors[axis]
    if size == 1:
        return blocks
    kind = blocks.dtype

    def pick(place):
        return lax.dynamic_slice_in_dim(blocks, jnp.clip(place, 0, size - 1), 1, axis)

    own = pick(coord).astype(F32)
    if size == 2:
        got = lax.ppermute(
            pick(1 - coord), "dp", pairs_of(factors, axis, lambda c: True, lambda c: 1 - c)
        )
        return (own + got.astype(F32)).astype(kind)
    upward, downward = None, None
    for step in range(1, size):
        away = size - step
        send_up, send_down = pick(coord + away), pick(coord - away)
        if upward is not None:
            send_up = (send_up.astype(F32) + upward.astype(F32)).astype(kind)
            send_down = (send_down.astype(F32) + downward.astype(F32)).astype(kind)
        upward = lax.ppermute(
            send_up, "dp", pairs_of(factors, axis, lambda c: c < step, lambda c: c + 1)
        )
        downward = lax.ppermute(
            send_down, "dp", pairs_of(factors, axis, lambda c: c >= away, lambda c: c - 1)
        )
    return (own + upward.astype(F32) + downward.astype(F32)).astype(kind)


def scatter_rows(full, factors, coords):
    n_axes = len(factors)
    total = 1
    for size in factors:
        total *= size
    rows = full.shape[0] // total
    half = rows // 2
    shaped = full.reshape(tuple(factors) + (rows, full.shape[1]))
    halves = []
    for part, order in ((0, range(n_axes - 1, 0, -1)), (1, range(1, n_axes))):
        block = lax.slice_in_dim(shaped, part * half, (part + 1) * half, axis=n_axes)
        for axis in (*order, 0):
            block = reduce_axis(block, factors, axis, coords[axis])
        halves.append(block.reshape(half, full.shape[1]))
    return jnp.concatenate(halves, 0)


def swap(value):
    return lax.ppermute(value, "tensor", [(0, 1), (1, 0)])


def join_tensor(mine, part, axis=0):
    other = swap(mine)
    return lax.dynamic_slice_in_dim(
        jnp.concatenate([other, mine, other], axis),
        (1 - part) * mine.shape[axis],
        2 * mine.shape[axis],
        axis,
    )


def split_tensor(value, part):
    half = value.shape[0] // 2
    give = lax.dynamic_slice_in_dim(value, (1 - part) * half, half, 0).astype(BF16)
    keep = lax.dynamic_slice_in_dim(value, part * half, half, 0).astype(F32)
    return keep + swap(give).astype(F32)


def rotate(values, cosine, sine):
    half_dim = values.shape[-1] // 2
    bshape = (values.shape[0],) + (1,) * (values.ndim - 2) + (half_dim,)
    cosine = cosine.reshape(bshape)
    sine = sine.reshape(bshape)
    first_half = values[..., :half_dim]
    second_half = values[..., half_dim:]
    return jnp.concatenate(
        [first_half * cosine - second_half * sine, second_half * cosine + first_half * sine], -1
    )


def seg_conv(values, taps, shift_bias, same_doc):
    n_rows = values.shape[0]
    n_taps = taps.shape[0]
    padded = jnp.pad(values, ((n_taps - 1, 0), (0, 0)))
    result = shift_bias[None, :] + taps[n_taps - 1][None, :] * values
    for offset in range(n_taps - 1):
        result = (
            result
            + taps[offset][None, :] * padded[offset : offset + n_rows] * same_doc[offset][:, None]
        )
    return result


def ssd_scan(inner, steps, decays, b_state, c_state, segment, block_len):
    n_rows, n_heads, head_dim = inner.shape
    n_blocks = n_rows // block_len
    x_blk = inner.reshape(n_blocks, block_len, n_heads, head_dim).transpose(0, 2, 1, 3)
    dt_blk = steps.reshape(n_blocks, block_len, n_heads).transpose(0, 2, 1)
    within = jnp.arange(block_len, dtype=jnp.int32)
    causal = within[:, None] >= within[None, :]
    cumul = jnp.einsum(
        "ts,csh->cht",
        causal.astype(F32),
        decays.reshape(n_blocks, block_len, n_heads),
        precision=EXACT,
    )
    b_blk = b_state.reshape(n_blocks, block_len, -1)
    c_blk = c_state.reshape(n_blocks, block_len, -1)
    seg_blk = segment.reshape(n_blocks, block_len)
    allowed = (seg_blk[:, :, None] == seg_blk[:, None, :]) & causal[None]
    differ = cumul[:, :, :, None] - cumul[:, :, None, :]
    kernel = jnp.exp(jnp.where(allowed[:, None], differ, -1e30))
    inner_prod = jnp.einsum("ctn,csn->cts", c_blk, b_blk, precision=PREC)
    x_step = x_blk * dt_blk[..., None]
    weights_ts = inner_prod[:, None] * kernel
    y_inner = jnp.einsum("chts,chsp->chtp", weights_ts, x_step, precision=PREC)
    last_seg = seg_blk[:, -1]
    to_end = (
        jnp.exp(cumul[:, :, -1:] - cumul)
        * (seg_blk == last_seg[:, None]).astype(F32)[:, None, :]
    )
    local_state = jnp.einsum(
        "chsp,csn->chpn", x_step * to_end[..., None], b_blk, precision=PREC
    )
    prev_seg = jnp.concatenate([jnp.full((1,), -1, dtype=jnp.int32), last_seg[:-1]])
    carry_keep = jnp.exp(cumul[:, :, -1]) * (last_seg == prev_seg).astype(F32)[:, None]
    state = jnp.zeros(local_state.shape[1:], F32)
    entering = [state]
    for block in range(n_blocks - 1):
        state = state * carry_keep[block][:, None, None] + local_state[block]
        entering.append(state)
    entering = jnp.stack(entering)
    from_start = jnp.exp(cumul) * (seg_blk == prev_seg[:, None]).astype(F32)[:, None, :]
    y_state = jnp.einsum("ctn,chpn->chtp", c_blk, entering, precision=PREC)
    total = y_inner + y_state * from_start[..., None]
    return total.transpose(0, 2, 1, 3).reshape(n_rows, n_heads * head_dim)


def mamba_core(
    gate_z,
    proj_x,
    proj_step,
    proj_bc,
    conv_w,
    conv_b,
    conv_s,
    conv_sb,
    log_decay,
    bias_step,
    gain_skip,
    gain_mix,
    segment,
    same_doc,
):
    n_rows, n_channels = gate_z.shape
    n_heads = proj_step.shape[1]
    head_dim = n_channels // n_heads
    x_conv = jax.nn.silu(seg_conv(proj_x, conv_w, conv_b, same_doc))
    bc_conv = jax.nn.silu(seg_conv(proj_bc, conv_s, conv_sb, same_doc))
    n_state = proj_bc.shape[1] // 2
    steps = jax.nn.softplus(proj_step + bias_step[None, :])
    decays = -steps * jnp.exp(log_decay)[None, :]
    ssm = ssd_scan(
        x_conv.reshape(n_rows, n_heads, head_dim),
        steps,
        decays,
        bc_conv[:, :n_state],
        bc_conv[:, n_state:],
        segment,
        BLK,
    )
    ssm = ssm + jnp.repeat(gain_skip, head_dim)[None, :] * x_conv
    gated = ssm * jax.nn.silu(gate_z)
    width = NGH * head_dim
    normed = []
    for first in range(0, n_channels, width):
        group = gated[:, first : first + width]
        normed.append(group * lax.rsqrt(jnp.mean(group * group, -1, keepdims=True) + EPS))
    return jnp.concatenate(normed, 1) * gain_mix[None, :]


def masked_scores(q_blk, keys, allowed, scaling):
    scores = jnp.einsum("tqd,sd->qts", q_blk, keys, preferred_element_type=F32) * scaling
    return jnp.where(allowed[None], scores, -1e30)


def query_blocks(segment):
    n_rows = segment.shape[0]
    q_len = min(QBLK, n_rows)
    index = jnp.arange(n_rows, dtype=jnp.int32)
    blocks = []
    for start in range(0, n_rows, q_len):
        stop = start + q_len
        allowed = (segment[start:stop, None] == segment[None, :stop]) & (
            index[start:stop, None] >= index[None, :stop]
        )
        blocks.append((start, stop, allowed))
    return blocks


def attend_forward(queries, keys, vals, blocks, scaling):
    outs, norms = [], []
    for start, stop, allowed in blocks:
        scores = masked_scores(queries[start:stop], keys[:stop], allowed, scaling)
        topmost = jnp.max(scores, -1, keepdims=True)
        expo = jnp.exp(scores - topmost)
        total = jnp.sum(expo, -1, keepdims=True)
        probs = (expo / total).astype(BF16)
        outs.append(jnp.einsum("qts,sd->tqd", probs, vals[:stop], preferred_element_type=F32))
        norms.append(topmost + jnp.log(total))
    return jnp.concatenate(outs, 0), norms


def attend_backward(queries, keys, vals, blocks, norms, grad_out, scaling):
    grad_q = []
    grad_keys = jnp.zeros(keys.shape, F32)
    grad_vals = jnp.zeros(vals.shape, F32)
    for (start, stop, allowed), norm in zip(blocks, norms):
        q_blk, dout = queries[start:stop], grad_out[start:stop]
        scores = masked_scores(q_blk, keys[:stop], allowed, scaling)
        probs = jnp.exp(scores - norm)
        dv = jnp.einsum("qts,tqd->sd", probs.astype(BF16), dout, preferred_element_type=F32)
        dprobs = jnp.einsum("tqd,sd->qts", dout, vals[:stop], preferred_element_type=F32)
        dscores = probs * (dprobs - jnp.sum(probs * dprobs, -1, keepdims=True))
        low = dscores.astype(BF16)
        grad_q.append(
            jnp.einsum("qts,sd->tqd", low, keys[:stop], preferred_element_type=F32) * scaling
        )
        dk = jnp.einsum("qts,tqd->sd", low, q_blk, preferred_element_type=F32) * scaling
        tail = ((0, keys.shape[0] - stop), (0, 0))
        grad_keys = grad_keys + jnp.pad(dk, tail)
        grad_vals = grad_vals + jnp.pad(dv, tail)
    return jnp.concatenate(grad_q, 0), grad_keys, grad_vals


def norm_back(grad_normed, unit_rows, inv_scale, gain):
    scaled = grad_normed * gain[None, :]
    return inv_scale * (scaled - unit_rows * jnp.mean(scaled * unit_rows, -1, keepdims=True))


def dot(a, b, dims):
    return lax.dot_general(a, b, (dims, ((), ())), preferred_element_type=F32)


def per_device(
    inputs,
    segments,
    cotangent,
    norm_gain,
    mix_in,
    step_in,
    state_in,
    conv_inner,
    conv_inner_bias,
    conv_state,
    conv_state_bias,
    decay_log,
    step_bias,
    skip_gain,
    mixer_gain,
    attn_in,
    mixer_out,
    attn_out,
    ffn_gain,
    ffn_in,
    ffn_down,
):
    part = lax.axis_index("tensor")
    place = lax.axis_index("dp")
    n_dp = lax.axis_size("dp")
    n_parts = lax.axis_size("tensor")
    factors = grid_of(n_dp)
    coords = coordinates(place, factors)
    rows = mix_in.shape[0]
    n_heads, twice = mix_in.shape[1:]
    head_dim = twice // 2
    inner = n_heads * head_dim
    n_rows = segments.shape[0]
    qkv_cols = attn_in.shape[1] * attn_in.shape[2]
    state_cols = state_in.shape[1]
    hid = ffn_down.shape[0]
    attn_cols = attn_out.shape[0] * attn_out.shape[1]
    d_model = inputs.shape[1]

    small_parts = (
        norm_gain,
        ffn_gain,
        conv_inner,
        conv_inner_bias,
        mixer_gain,
        conv_state,
        conv_state_bias,
    )
    small = jnp.concatenate([a.reshape(-1) for a in small_parts] + [state_in.reshape(-1)])
    n_small = small.shape[0] - state_in.size
    both = join_tensor(small.reshape(1, -1), part)
    state_rows = both[:, n_small:].reshape(rows, state_cols)
    small_cols = -(-n_parts * n_small // rows)
    small_block = jnp.pad(
        both[:, :n_small].reshape(-1), (0, rows * small_cols - n_parts * n_small)
    ).reshape(rows, small_cols)
    step_cols = -(-(n_heads + small_cols) // 128) * 128
    step_block = jnp.pad(
        jnp.concatenate([step_in, small_block], 1),
        ((0, 0), (0, step_cols - n_heads - small_cols)),
    )
    front = jnp.concatenate(
        [
            mix_in[..., :head_dim].reshape(rows, inner),
            mix_in[..., head_dim:].reshape(rows, inner),
            attn_in.reshape(rows, qkv_cols),
            state_rows,
            step_block,
        ],
        1,
    )
    back = jnp.concatenate(
        [
            mixer_out.reshape(inner, rows).T,
            attn_out.reshape(attn_cols, rows).T,
            ffn_in.reshape(rows, 2 * hid),
            ffn_down.T,
        ],
        1,
    )
    x_at, qkv_at = inner, 2 * inner
    bc_at = qkv_at + qkv_cols
    step_at = bc_at + state_cols
    front_full = gather_rows(front, factors, coords)
    front_full, back = lax.optimization_barrier((front_full, back))
    back_full = gather_rows(back, factors, coords)
    mixout_t = back_full[:, :inner]
    attnout_t = back_full[:, inner : inner + attn_cols]
    ffin_full = back_full[:, inner + attn_cols : inner + attn_cols + 2 * hid]
    down_t = back_full[:, inner + attn_cols + 2 * hid :]

    smalls = front_full.reshape(n_dp, rows, -1)[
        :, :, step_at + n_heads : step_at + n_heads + small_cols
    ]
    smalls = smalls.reshape(n_dp, -1)[:, : n_parts * n_small].reshape(n_dp * n_parts, n_small)
    smalls = smalls.astype(F32)
    pieces = []
    at = 0
    for item in small_parts:
        piece = smalls[:, at : at + item.size].reshape((-1,) + item.shape)
        at += item.size
        if item.ndim == 2:
            piece = piece.transpose(1, 0, 2).reshape(item.shape[0], -1)
        else:
            piece = piece.reshape(-1)
        pieces.append(piece)
    gain_first, gain_second, conv_full, conv_bias_full, gain_mix_full, conv_bc, conv_bc_bias = pieces

    def local_cols(array, axis_dim):
        return lax.dynamic_slice_in_dim(array, part * inner, inner, axis_dim)

    def widen(local, axis_dim):
        full_shape = list(local.shape)
        full_shape[axis_dim] = inner * n_parts
        return lax.dynamic_update_slice_in_dim(
            jnp.zeros(full_shape, F32), local, part * inner, axis_dim
        )

    conv_local = local_cols(conv_full, 1)
    conv_bias_local = local_cols(conv_bias_full, 0)
    gain_mixer = local_cols(gain_mix_full, 0)

    cot_full = join_tensor(cotangent, part)
    inputs_f = inputs.astype(F32)
    inv_first = lax.rsqrt(jnp.mean(inputs_f * inputs_f, -1, keepdims=True) + EPS)
    unit_first = inputs_f * inv_first
    normed = join_tensor((unit_first * gain_first[None, :]).astype(BF16), part)

    row_index = jnp.arange(n_rows, dtype=jnp.int32)
    places = place * n_rows + row_index - segments
    half_dim = ADIM // 2
    freqs = ROPE_BASE ** (-2.0 * jnp.arange(half_dim, dtype=F32) / ADIM)
    angles = places.astype(F32)[:, None] * freqs[None, :]
    cosine, sine = jnp.cos(angles), jnp.sin(angles)
    n_taps = conv_inner.shape[0]
    same_doc = [(places >= n_taps - 1 - k).astype(F32) for k in range(n_taps - 1)]

    proj = dot(normed, front_full, ((1,), (0,)))

    def mixer(*values):
        return mamba_core(*values, segments, same_doc)

    mamba_value, mamba_pull = jax.vjp(
        mixer,
        proj[:, :inner],
        proj[:, x_at:qkv_at],
        proj[:, step_at : step_at + n_heads],
        proj[:, bc_at:step_at],
        conv_local,
        conv_bias_local,
        conv_bc,
        conv_bc_bias,
        decay_log,
        step_bias,
        skip_gain,
        gain_mixer,
    )
    mamba_low = mamba_value.astype(BF16)
    scaling = ADIM ** (-0.5)
    q_cols = QPK * ADIM
    q_part = proj[:, qkv_at : qkv_at + q_cols].reshape(n_rows, QPK, ADIM)
    k_part = proj[:, qkv_at + q_cols : qkv_at + q_cols + ADIM]
    queries = rotate(q_part, cosine, sine).astype(BF16)
    keys = rotate(k_part, cosine, sine).astype(BF16)
    vals = proj[:, qkv_at + q_cols + ADIM : bc_at].astype(BF16)
    blocks = query_blocks(segments)
    attended, norms = attend_forward(queries, keys, vals, blocks, scaling)
    attended_low = attended.reshape(n_rows, attn_cols).astype(BF16)
    mix_low = jnp.concatenate([mamba_low, attended_low], 1)
    out_t = back_full[:, : inner + attn_cols]
    mixed = split_tensor(dot(mix_low, out_t, ((1,), (1,))), part)
    middle = inputs_f + mixed
    inv_second = lax.rsqrt(jnp.mean(middle * middle, -1, keepdims=True) + EPS)
    unit_second = middle * inv_second
    hidden = join_tensor((unit_second * gain_second[None, :]).astype(BF16), part)
    gate_up = dot(hidden, ffin_full, ((1,), (0,)))
    gate = gate_up[:, :hid]
    upper = gate_up[:, hid:]
    sigma = jax.nn.sigmoid(gate)
    active = (gate * sigma * upper).astype(BF16)
    ffn_value = split_tensor(dot(active, down_t, ((1,), (1,))), part)
    output = (middle + ffn_value).astype(BF16)

    grad_down = dot(cot_full, active, ((0,), (0,)))
    grad_active = dot(cot_full, down_t, ((1,), (0,)))
    grad_gate = grad_active * upper * sigma * (1.0 + gate * (1.0 - sigma))
    grad_up = grad_active * gate * sigma
    grad_gu = jnp.concatenate([grad_gate.astype(BF16), grad_up.astype(BF16)], 1)
    grad_ffin = dot(hidden, grad_gu, ((0,), (0,)))
    ffn_sum = scatter_rows(
        jnp.concatenate([grad_ffin.astype(BF16), grad_down.astype(BF16)], 1), factors, coords
    ).astype(F32)
    grad_hidden = split_tensor(dot(grad_gu, ffin_full, ((1,), (1,))), part)
    grad_gain_second = jnp.sum(grad_hidden * unit_second, 0)
    grad_middle = cotangent.astype(F32) + norm_back(
        grad_hidden, unit_second, inv_second, gain_second
    )
    grad_mixed = join_tensor(grad_middle.astype(BF16), part)
    out_sum = scatter_rows(
        dot(grad_mixed, mix_low, ((0,), (0,))).astype(BF16), factors, coords
    ).astype(F32)
    grad_att = dot(grad_mixed, attnout_t, ((1,), (0,))).astype(BF16)
    grad_mamba = dot(grad_mixed, mixout_t, ((1,), (0,)))
    grad_q, grad_k, grad_v = attend_backward(
        queries, keys, vals, blocks, norms, grad_att.reshape(n_rows, QPK, ADIM), scaling
    )
    grad_q = rotate(grad_q, cosine, -sine).reshape(n_rows, q_cols)
    grad_k = rotate(grad_k, cosine, -sine)
    (
        grad_z,
        grad_x,
        grad_step,
        grad_bc,
        grad_conv,
        grad_conv_bias,
        grad_conv_bc,
        grad_conv_bc_bias,
        grad_decay,
        grad_step_bias,
        grad_skip,
        grad_gain_mix,
    ) = mamba_pull(grad_mamba)
    grad_proj = jnp.concatenate(
        [
            grad_z.astype(BF16),
            grad_x.astype(BF16),
            grad_q.astype(BF16),
            grad_k.astype(BF16),
            grad_v.astype(BF16),
            grad_bc.astype(BF16),
            grad_step.astype(BF16),
            jnp.zeros((n_rows, step_cols - n_heads), BF16),
        ],
        1,
    )
    front_sum = scatter_rows(
        dot(normed, grad_proj, ((0,), (0,))).astype(BF16), factors, coords
    ).astype(F32)
    grad_normed = split_tensor(dot(grad_proj, front_full, ((1,), (1,))), part)
    grad_gain_first = jnp.sum(grad_normed * unit_first, 0)
    inputs_grad = grad_middle + norm_back(grad_normed, unit_first, inv_first, gain_first)

    small_grads = (
        grad_gain_first,
        grad_gain_second,
        widen(grad_conv, 1),
        widen(grad_conv_bias, 0),
        widen(grad_gain_mix, 0),
        grad_conv_bc,
        grad_conv_bc_bias,
    )
    columns = []
    for item, grad in zip(small_parts, small_grads):
        if item.ndim == 2:
            piece = grad.reshape(item.shape[0], n_dp * n_parts, -1).transpose(1, 0, 2)
        else:
            piece = grad
        columns.append(piece.reshape(n_dp * n_parts, -1))
    piece_rows = jnp.concatenate(columns, 1).reshape(n_dp, n_parts * n_small)
    heads = jnp.concatenate([grad_decay, grad_step_bias, grad_skip])
    filled = n_parts * n_small + heads.shape[0]
    lines = -(-filled // 1024) * 8
    packed = jnp.concatenate(
        [
            piece_rows,
            jnp.broadcast_to(heads[None, :], (n_dp, heads.shape[0])),
            jnp.zeros((n_dp, lines * 128 - filled), F32),
        ],
        1,
    ).reshape(tuple(factors) + (lines, 128))
    for axis in range(len(factors)):
        packed = reduce_axis(packed, factors, axis, coords[axis])
    packed = packed.reshape(-1)
    pair = packed[: n_parts * n_small].reshape(n_parts, n_small)
    mine = lax.dynamic_index_in_dim(pair, part, 0, keepdims=False) + swap(
        lax.dynamic_index_in_dim(pair, 1 - part, 0, keepdims=False)
    )
    small_out = []
    at = 0
    for item in small_parts:
        small_out.append(mine[at : at + item.size].reshape(item.shape))
        at += item.size
    head_sums = packed[n_parts * n_small : filled].reshape(3, n_heads)

    state_sum = front_sum[:, bc_at:step_at]
    half = rows // n_parts
    state_grad = lax.dynamic_slice_in_dim(state_sum, part * half, half, 0) + swap(
        lax.dynamic_slice_in_dim(state_sum, (1 - part) * half, half, 0)
    )
    mix_grad = jnp.concatenate(
        [
            front_sum[:, :inner].reshape(rows, n_heads, head_dim),
            front_sum[:, x_at:qkv_at].reshape(rows, n_heads, head_dim),
        ],
        -1,
    )
    return (
        output,
        inputs_grad,
        small_out[0],
        mix_grad,
        front_sum[:, step_at : step_at + n_heads],
        state_grad,
        small_out[2],
        small_out[3],
        small_out[5],
        small_out[6],
        head_sums[0],
        head_sums[1],
        head_sums[2],
        small_out[4],
        front_sum[:, qkv_at:bc_at].reshape(attn_in.shape),
        out_sum[:, :inner].T.reshape(mixer_out.shape),
        out_sum[:, inner:].T.reshape(attn_out.shape),
        small_out[1],
        ffn_sum[:, : 2 * hid].reshape(ffn_in.shape),
        ffn_sum[:, 2 * hid :].T,
    )


def solution(mesh):
    return jax.shard_map(
        per_device,
        mesh=mesh,
        in_specs=(
            P(("dp", "tensor"), None),
            P("dp"),
            P(("dp", "tensor"), None),
            P(("dp", "tensor")),
            P("dp", "tensor", None),
            P("dp", "tensor"),
            P(("dp", "tensor"), None),
            P(None, ("dp", "tensor")),
            P(("dp", "tensor")),
            P(None, ("dp", "tensor")),
            P(("dp", "tensor")),
            P("tensor"),
            P("tensor"),
            P("tensor"),
            P(("dp", "tensor")),
            P("dp", "tensor", None),
            P("tensor", None, "dp"),
            P("tensor", None, "dp"),
            P(("dp", "tensor")),
            P("dp", None, "tensor"),
            P("tensor", "dp"),
        ),
        out_specs=(
            P(("dp", "tensor"), None),
            P(("dp", "tensor"), None),
            P(("dp", "tensor")),
            P("dp", "tensor", None),
            P("dp", "tensor"),
            P(("dp", "tensor"), None),
            P(None, ("dp", "tensor")),
            P(("dp", "tensor")),
            P(None, ("dp", "tensor")),
            P(("dp", "tensor")),
            P("tensor"),
            P("tensor"),
            P("tensor"),
            P(("dp", "tensor")),
            P("dp", "tensor", None),
            P("tensor", None, "dp"),
            P("tensor", None, "dp"),
            P(("dp", "tensor")),
            P("dp", None, "tensor"),
            P("tensor", "dp"),
        ),
        check_vma=False,
    )
```

```python
import jax
import jax.numpy as jnp
from jax import lax
from jax.sharding import PartitionSpec as P

QPK = 4
ADIM = 64
NGH = 12
BLK = 256
QBLK = 512

PREC = lax.Precision.DEFAULT
EXACT = lax.Precision.HIGHEST
EPS = 1e-05
ROPE_BASE = 100000000000.0
F32 = jnp.float32
BF16 = jnp.bfloat16


def grid_of(size):
    factors = []
    while size > 1:
        factors.append(2)
        size //= 2
    return tuple(factors)


def coordinates(index, factors):
    coords = []
    for size in reversed(factors):
        coords.append(index % size)
        index = index // size
    return coords[::-1]


def exchange(value, factors, axis):
    stride = 2 ** (len(factors) - 1 - axis)
    pairs = [(index, index ^ stride) for index in range(2 ** len(factors))]
    return lax.ppermute(value, "dp", pairs)


def gather_axis(block, factors, coords, axis):
    other = exchange(block, factors, axis)
    return lax.dynamic_slice_in_dim(
        jnp.concatenate([other, block, other], axis), 1 - coords[axis], 2, axis
    )


def gather_block(block, factors, coords, axes):
    for axis in axes:
        block = gather_axis(block, factors, coords, axis)
    return block


def gather_first(block, factors, coords, cut):
    n_axes = len(factors)
    first, second = block[..., :cut], block[..., cut:]
    first = gather_axis(first, factors, coords, n_axes - 2)
    second = gather_axis(second, factors, coords, n_axes - 1)
    return first, second


def gather_second(first, second, factors, coords):
    n_axes = len(factors)
    first = gather_axis(first, factors, coords, n_axes - 1)
    second = gather_axis(second, factors, coords, n_axes - 2)
    return first.reshape(-1, first.shape[-1]), second.reshape(-1, second.shape[-1])


def reduce_axis(blocks, factors, coords, axis):
    def pick(place):
        return lax.dynamic_slice_in_dim(blocks, place, 1, axis)

    got = exchange(pick(1 - coords[axis]), factors, axis)
    return (pick(coords[axis]).astype(F32) + got.astype(F32)).astype(blocks.dtype)


def scatter_first(first, second, factors, coords):
    n_axes = len(factors)
    rows = first.shape[0] // 2**n_axes
    first = first.reshape(tuple(factors) + (rows, first.shape[1]))
    second = second.reshape(tuple(factors) + (rows, second.shape[1]))
    first = reduce_axis(first, factors, coords, n_axes - 1)
    second = reduce_axis(second, factors, coords, n_axes - 2)
    return first, second


def scatter_second(first, second, factors, coords):
    n_axes = len(factors)
    first = reduce_axis(first, factors, coords, n_axes - 2)
    second = reduce_axis(second, factors, coords, n_axes - 1)
    return jnp.concatenate([first, second], n_axes + 1)


def scatter_block(block, factors, coords, axes):
    for axis in axes:
        block = reduce_axis(block, factors, coords, axis)
    return block


def tie(values):
    return lax.optimization_barrier(values)


def swap(value):
    return lax.ppermute(value, "tensor", [(0, 1), (1, 0)])


def join_tensor(mine, part, axis=0):
    other = swap(mine)
    return lax.dynamic_slice_in_dim(
        jnp.concatenate([other, mine, other], axis),
        (1 - part) * mine.shape[axis],
        2 * mine.shape[axis],
        axis,
    )


def split_tensor(value, part):
    half = value.shape[0] // 2
    give = lax.dynamic_slice_in_dim(value, (1 - part) * half, half, 0).astype(BF16)
    keep = lax.dynamic_slice_in_dim(value, part * half, half, 0).astype(F32)
    return keep + swap(give).astype(F32)


def rotate(values, cosine, sine):
    half_dim = values.shape[-1] // 2
    bshape = (values.shape[0],) + (1,) * (values.ndim - 2) + (half_dim,)
    cosine = cosine.reshape(bshape)
    sine = sine.reshape(bshape)
    first_half = values[..., :half_dim]
    second_half = values[..., half_dim:]
    return jnp.concatenate(
        [first_half * cosine - second_half * sine, second_half * cosine + first_half * sine], -1
    )


def seg_conv(values, taps, shift_bias, same_doc):
    n_rows = values.shape[0]
    n_taps = taps.shape[0]
    padded = jnp.pad(values, ((n_taps - 1, 0), (0, 0)))
    result = shift_bias[None, :] + taps[n_taps - 1][None, :] * values
    for offset in range(n_taps - 1):
        result = (
            result
            + taps[offset][None, :] * padded[offset : offset + n_rows] * same_doc[offset][:, None]
        )
    return result


def ssd_scan(inner, steps, decays, b_state, c_state, segment, block_len):
    n_rows, n_heads, head_dim = inner.shape
    n_blocks = n_rows // block_len
    x_blk = inner.reshape(n_blocks, block_len, n_heads, head_dim).transpose(0, 2, 1, 3)
    dt_blk = steps.reshape(n_blocks, block_len, n_heads).transpose(0, 2, 1)
    within = jnp.arange(block_len, dtype=jnp.int32)
    causal = within[:, None] >= within[None, :]
    cumul = jnp.einsum(
        "ts,csh->cht",
        causal.astype(F32),
        decays.reshape(n_blocks, block_len, n_heads),
        precision=EXACT,
    )
    b_blk = b_state.reshape(n_blocks, block_len, -1)
    c_blk = c_state.reshape(n_blocks, block_len, -1)
    seg_blk = segment.reshape(n_blocks, block_len)
    allowed = (seg_blk[:, :, None] == seg_blk[:, None, :]) & causal[None]
    differ = cumul[:, :, :, None] - cumul[:, :, None, :]
    kernel = jnp.exp(jnp.where(allowed[:, None], differ, -1e30))
    inner_prod = jnp.einsum("ctn,csn->cts", c_blk, b_blk, precision=PREC)
    x_step = x_blk * dt_blk[..., None]
    weights_ts = inner_prod[:, None] * kernel
    y_inner = jnp.einsum("chts,chsp->chtp", weights_ts, x_step, precision=PREC)
    last_seg = seg_blk[:, -1]
    to_end = (
        jnp.exp(cumul[:, :, -1:] - cumul)
        * (seg_blk == last_seg[:, None]).astype(F32)[:, None, :]
    )
    local_state = jnp.einsum(
        "chsp,csn->chpn", x_step * to_end[..., None], b_blk, precision=PREC
    )
    prev_seg = jnp.concatenate([jnp.full((1,), -1, dtype=jnp.int32), last_seg[:-1]])
    carry_keep = jnp.exp(cumul[:, :, -1]) * (last_seg == prev_seg).astype(F32)[:, None]
    state = jnp.zeros(local_state.shape[1:], F32)
    entering = [state]
    for block in range(n_blocks - 1):
        state = state * carry_keep[block][:, None, None] + local_state[block]
        entering.append(state)
    entering = jnp.stack(entering)
    from_start = jnp.exp(cumul) * (seg_blk == prev_seg[:, None]).astype(F32)[:, None, :]
    y_state = jnp.einsum("ctn,chpn->chtp", c_blk, entering, precision=PREC)
    total = y_inner + y_state * from_start[..., None]
    return total.transpose(0, 2, 1, 3).reshape(n_rows, n_heads * head_dim)


def mamba_inputs(
    proj_x, proj_step, proj_bc, conv_w, conv_b, conv_s, conv_sb, log_decay, bias_step, same_doc
):
    x_conv = jax.nn.silu(seg_conv(proj_x, conv_w, conv_b, same_doc))
    bc_conv = jax.nn.silu(seg_conv(proj_bc, conv_s, conv_sb, same_doc))
    steps = jax.nn.softplus(proj_step + bias_step[None, :])
    decays = -steps * jnp.exp(log_decay)[None, :]
    return x_conv, bc_conv, steps, decays


def mamba_scan(x_conv, bc_conv, steps, decays, segment):
    n_rows, n_heads = steps.shape
    n_state = bc_conv.shape[1] // 2
    return ssd_scan(
        x_conv.reshape(n_rows, n_heads, -1),
        steps,
        decays,
        bc_conv[:, :n_state],
        bc_conv[:, n_state:],
        segment,
        BLK,
    )


def mamba_gate(ssm, x_conv, gate_z, gain_skip, gain_mix):
    n_channels = gate_z.shape[1]
    head_dim = n_channels // gain_skip.shape[0]
    ssm = ssm + jnp.repeat(gain_skip, head_dim)[None, :] * x_conv
    gated = ssm * jax.nn.silu(gate_z)
    width = NGH * head_dim
    normed = []
    for first in range(0, n_channels, width):
        group = gated[:, first : first + width]
        normed.append(group * lax.rsqrt(jnp.mean(group * group, -1, keepdims=True) + EPS))
    return jnp.concatenate(normed, 1) * gain_mix[None, :]


def masked_scores(q_blk, keys, allowed, scaling):
    scores = jnp.einsum("tqd,sd->qts", q_blk, keys, preferred_element_type=F32) * scaling
    return jnp.where(allowed[None], scores, -1e30)


def query_blocks(segment):
    n_rows = segment.shape[0]
    q_len = min(QBLK, n_rows)
    index = jnp.arange(n_rows, dtype=jnp.int32)
    blocks = []
    for start in range(0, n_rows, q_len):
        stop = start + q_len
        allowed = (segment[start:stop, None] == segment[None, :stop]) & (
            index[start:stop, None] >= index[None, :stop]
        )
        blocks.append((start, stop, allowed))
    return blocks


def attend_forward(queries, keys, vals, blocks, scaling):
    outs, norms = [], []
    for start, stop, allowed in blocks:
        scores = masked_scores(queries[start:stop], keys[:stop], allowed, scaling)
        topmost = jnp.max(scores, -1, keepdims=True)
        expo = jnp.exp(scores - topmost)
        total = jnp.sum(expo, -1, keepdims=True)
        probs = (expo / total).astype(BF16)
        outs.append(jnp.einsum("qts,sd->tqd", probs, vals[:stop], preferred_element_type=F32))
        norms.append(topmost + jnp.log(total))
    return jnp.concatenate(outs, 0), norms


def attend_backward(queries, keys, vals, blocks, norms, grad_out, scaling):
    grad_q = []
    grad_keys = jnp.zeros(keys.shape, F32)
    grad_vals = jnp.zeros(vals.shape, F32)
    for (start, stop, allowed), norm in zip(blocks, norms):
        q_blk, dout = queries[start:stop], grad_out[start:stop]
        scores = masked_scores(q_blk, keys[:stop], allowed, scaling)
        probs = jnp.exp(scores - norm)
        dv = jnp.einsum("qts,tqd->sd", probs.astype(BF16), dout, preferred_element_type=F32)
        dprobs = jnp.einsum("tqd,sd->qts", dout, vals[:stop], preferred_element_type=F32)
        dscores = probs * (dprobs - jnp.sum(probs * dprobs, -1, keepdims=True))
        low = dscores.astype(BF16)
        grad_q.append(
            jnp.einsum("qts,sd->tqd", low, keys[:stop], preferred_element_type=F32) * scaling
        )
        dk = jnp.einsum("qts,tqd->sd", low, q_blk, preferred_element_type=F32) * scaling
        tail = ((0, keys.shape[0] - stop), (0, 0))
        grad_keys = grad_keys + jnp.pad(dk, tail)
        grad_vals = grad_vals + jnp.pad(dv, tail)
    return jnp.concatenate(grad_q, 0), grad_keys, grad_vals


def norm_back(grad_normed, unit_rows, inv_scale, gain):
    scaled = grad_normed * gain[None, :]
    return inv_scale * (scaled - unit_rows * jnp.mean(scaled * unit_rows, -1, keepdims=True))


def dot(a, b, dims):
    return lax.dot_general(a, b, (dims, ((), ())), preferred_element_type=F32)


def per_device(
    inputs,
    segments,
    cotangent,
    norm_gain,
    mix_in,
    step_in,
    state_in,
    conv_inner,
    conv_inner_bias,
    conv_state,
    conv_state_bias,
    decay_log,
    step_bias,
    skip_gain,
    mixer_gain,
    attn_in,
    mixer_out,
    attn_out,
    ffn_gain,
    ffn_in,
    ffn_down,
):
    part = lax.axis_index("tensor")
    place = lax.axis_index("dp")
    n_dp = lax.axis_size("dp")
    n_parts = lax.axis_size("tensor")
    factors = grid_of(n_dp)
    coords = coordinates(place, factors)
    rows = mix_in.shape[0]
    n_heads, twice = mix_in.shape[1:]
    head_dim = twice // 2
    inner = n_heads * head_dim
    n_rows = segments.shape[0]
    qkv_cols = attn_in.shape[1] * attn_in.shape[2]
    state_cols = state_in.shape[1]
    hid = ffn_down.shape[0]
    attn_cols = attn_out.shape[0] * attn_out.shape[1]
    d_model = inputs.shape[1]

    small_parts = (
        norm_gain,
        ffn_gain,
        conv_inner,
        conv_inner_bias,
        mixer_gain,
        conv_state,
        conv_state_bias,
    )
    small = jnp.concatenate([a.reshape(-1) for a in small_parts] + [state_in.reshape(-1)])
    n_small = small.shape[0] - state_in.size
    both = join_tensor(small.reshape(1, -1), part)
    state_rows = both[:, n_small:].reshape(rows, state_cols)
    small_cols = -(-n_parts * n_small // rows)
    small_block = jnp.pad(
        both[:, :n_small].reshape(-1), (0, rows * small_cols - n_parts * n_small)
    ).reshape(rows, small_cols)
    step_cols = -(-n_heads // 128) * 128
    pad_cols = -(-small_cols // 128) * 128
    side = jnp.concatenate(
        [state_rows, jnp.pad(small_block, ((0, 0), (0, pad_cols - small_cols)))], 1
    )
    front = jnp.concatenate(
        [
            mix_in[..., :head_dim].reshape(rows, inner),
            attn_in.reshape(rows, qkv_cols),
            mix_in[..., head_dim:].reshape(rows, inner),
            jnp.pad(step_in, ((0, 0), (0, step_cols - n_heads))),
        ],
        1,
    )
    back = jnp.concatenate(
        [
            mixer_out.reshape(inner, rows).T,
            attn_out.reshape(attn_cols, rows).T,
            ffn_down.T,
            ffn_in.reshape(rows, 2 * hid),
        ],
        1,
    )
    early_cols = inner + qkv_cols
    n_axes = len(factors)
    outer = range(n_axes - 2)
    inward = range(n_axes - 3, -1, -1)

    def as_block(shard):
        return shard.reshape((1,) * n_axes + shard.shape)

    front_block = gather_block(as_block(front), factors, coords, outer)
    early_w, late_w = gather_second(
        *gather_first(front_block, factors, coords, early_cols), factors, coords
    )
    side_w = gather_block(as_block(side), factors, coords, range(n_axes))
    side_w = side_w.reshape(-1, side.shape[1])
    early_w, late_w, side_w, back = tie((early_w, late_w, side_w, back))
    out_cols = inner + attn_cols
    state_w = side_w[:, :state_cols]

    smalls = side_w.reshape(n_dp, rows, -1)[:, :, state_cols : state_cols + small_cols]
    smalls = smalls.reshape(n_dp, -1)[:, : n_parts * n_small].reshape(n_dp * n_parts, n_small)
    smalls = smalls.astype(F32)
    pieces = []
    at = 0
    for item in small_parts:
        piece = smalls[:, at : at + item.size].reshape((-1,) + item.shape)
        at += item.size
        if item.ndim == 2:
            piece = piece.transpose(1, 0, 2).reshape(item.shape[0], -1)
        else:
            piece = piece.reshape(-1)
        pieces.append(piece)
    gain_first, gain_second, conv_full, conv_bias_full, gain_mix_full, conv_bc, conv_bc_bias = pieces

    def local_cols(array, axis_dim):
        return lax.dynamic_slice_in_dim(array, part * inner, inner, axis_dim)

    def widen(local, axis_dim):
        full_shape = list(local.shape)
        full_shape[axis_dim] = inner * n_parts
        return lax.dynamic_update_slice_in_dim(
            jnp.zeros(full_shape, F32), local, part * inner, axis_dim
        )

    conv_local = local_cols(conv_full, 1)
    conv_bias_local = local_cols(conv_bias_full, 0)
    gain_mixer = local_cols(gain_mix_full, 0)

    cot_full = join_tensor(cotangent, part)
    inputs_f = inputs.astype(F32)
    inv_first = lax.rsqrt(jnp.mean(inputs_f * inputs_f, -1, keepdims=True) + EPS)
    unit_first = inputs_f * inv_first
    normed = join_tensor((unit_first * gain_first[None, :]).astype(BF16), part)

    row_index = jnp.arange(n_rows, dtype=jnp.int32)
    places = place * n_rows + row_index - segments
    half_dim = ADIM // 2
    freqs = ROPE_BASE ** (-2.0 * jnp.arange(half_dim, dtype=F32) / ADIM)
    angles = places.astype(F32)[:, None] * freqs[None, :]
    cosine, sine = jnp.cos(angles), jnp.sin(angles)
    n_taps = conv_inner.shape[0]
    same_doc = [(places >= n_taps - 1 - k).astype(F32) for k in range(n_taps - 1)]

    proj_early = dot(normed, early_w, ((1,), (0,)))
    proj_late = dot(normed, late_w, ((1,), (0,)))
    proj_bc = dot(normed, state_w, ((1,), (0,)))

    back_block = gather_block(as_block(back), factors, coords, outer[:1])

    def inputs_of(*values):
        return mamba_inputs(*values, same_doc)

    def scan_of(*values):
        return mamba_scan(*values, segments)

    (x_conv, bc_conv, steps, decays), inputs_pull = jax.vjp(
        inputs_of,
        proj_late[:, :inner],
        proj_late[:, inner : inner + n_heads],
        proj_bc,
        conv_local,
        conv_bias_local,
        conv_bc,
        conv_bc_bias,
        decay_log,
        step_bias,
    )
    scaling = ADIM ** (-0.5)
    q_cols = QPK * ADIM
    q_part = proj_early[:, inner : inner + q_cols].reshape(n_rows, QPK, ADIM)
    k_part = proj_early[:, inner + q_cols : inner + q_cols + ADIM]
    queries = rotate(q_part, cosine, sine).astype(BF16)
    keys = rotate(k_part, cosine, sine).astype(BF16)
    vals = proj_early[:, inner + q_cols + ADIM :].astype(BF16)
    blocks = query_blocks(segments)
    queries, back_block = tie((queries, back_block))
    back_block = gather_block(back_block, factors, coords, outer[1:])
    attended, norms = attend_forward(queries, keys, vals, blocks, scaling)
    attended_low = attended.reshape(n_rows, attn_cols).astype(BF16)
    back_block, x_conv, attended_low = tie((back_block, x_conv, attended_low))
    half_heads = n_heads // 2
    half_inner = inner // 2

    def halves_of(value, size):
        return value[:, :size], value[:, size:]

    x_two = halves_of(x_conv, half_inner)
    step_two = halves_of(steps, half_heads)
    decay_two = halves_of(decays, half_heads)
    back_first, back_second = gather_first(back_block, factors, coords, out_cols + hid)
    ssm_one, scan_pull_one = jax.vjp(scan_of, x_two[0], bc_conv, step_two[0], decay_two[0])
    back_first, back_second, ssm_one, x_next = tie((back_first, back_second, ssm_one, x_two[1]))
    outs_w, ffin_full = gather_second(back_first, back_second, factors, coords)
    mixout_t = outs_w[:, :inner]
    attnout_t = outs_w[:, inner:out_cols]
    out_t = outs_w[:, :out_cols]
    down_t = outs_w[:, out_cols:]
    ssm_two, scan_pull_two = jax.vjp(scan_of, x_next, bc_conv, step_two[1], decay_two[1])
    mamba_value, gate_pull = jax.vjp(
        mamba_gate,
        jnp.concatenate([ssm_one, ssm_two], 1),
        x_conv,
        proj_early[:, :inner],
        skip_gain,
        gain_mixer,
    )
    mamba_low = mamba_value.astype(BF16)
    mix_low = jnp.concatenate([mamba_low, attended_low], 1)
    mixed = split_tensor(dot(mix_low, out_t, ((1,), (1,))), part)
    middle = inputs_f + mixed
    inv_second = lax.rsqrt(jnp.mean(middle * middle, -1, keepdims=True) + EPS)
    unit_second = middle * inv_second
    hidden = join_tensor((unit_second * gain_second[None, :]).astype(BF16), part)
    gate_up = dot(hidden, ffin_full, ((1,), (0,)))
    gate = gate_up[:, :hid]
    upper = gate_up[:, hid:]
    sigma = jax.nn.sigmoid(gate)
    active = (gate * sigma * upper).astype(BF16)
    ffn_value = split_tensor(dot(active, down_t, ((1,), (1,))), part)
    output = (middle + ffn_value).astype(BF16)

    grad_down = dot(cot_full, active, ((0,), (0,)))
    grad_active = dot(cot_full, down_t, ((1,), (0,)))
    grad_gate = grad_active * upper * sigma * (1.0 + gate * (1.0 - sigma))
    grad_up = grad_active * gate * sigma
    grad_gu = jnp.concatenate([grad_gate.astype(BF16), grad_up.astype(BF16)], 1)
    grad_ffin = dot(hidden, grad_gu, ((0,), (0,)))
    grad_hidden = split_tensor(dot(grad_gu, ffin_full, ((1,), (1,))), part)
    grad_gain_second = jnp.sum(grad_hidden * unit_second, 0)
    grad_middle = cotangent.astype(F32) + norm_back(
        grad_hidden, unit_second, inv_second, gain_second
    )
    grad_mixed = join_tensor(grad_middle.astype(BF16), part)
    grad_outs = dot(grad_mixed, mix_low, ((0,), (0,)))
    back_first, back_second = scatter_first(
        grad_ffin.astype(BF16),
        jnp.concatenate([grad_down.astype(BF16), grad_outs.astype(BF16)], 1),
        factors,
        coords,
    )
    grad_att = dot(grad_mixed, attnout_t, ((1,), (0,))).astype(BF16)
    grad_mamba = dot(grad_mixed, mixout_t, ((1,), (0,)))
    grad_q, grad_k, grad_v = attend_backward(
        queries, keys, vals, blocks, norms, grad_att.reshape(n_rows, QPK, ADIM), scaling
    )
    grad_q = rotate(grad_q, cosine, -sine).reshape(n_rows, q_cols)
    grad_k = rotate(grad_k, cosine, -sine)
    grad_ssm, grad_xc, grad_z, grad_skip, grad_gain_mix = gate_pull(grad_mamba)
    grad_early = jnp.concatenate(
        [
            grad_z.astype(BF16),
            grad_q.astype(BF16),
            grad_k.astype(BF16),
            grad_v.astype(BF16),
        ],
        1,
    )
    early_full = dot(normed, grad_early, ((0,), (0,))).astype(BF16)
    early_half = early_cols // 256 * 128
    early_full, back_first, back_second, grad_ssm = tie(
        (early_full, back_first, back_second, grad_ssm)
    )
    back_block = scatter_second(back_first, back_second, factors, coords)
    early_first, early_second = scatter_first(
        early_full[:, :early_half], early_full[:, early_half:], factors, coords
    )
    grad_ssm_two = halves_of(grad_ssm, half_inner)
    one = scan_pull_one(grad_ssm_two[0])
    one, back_block, early_first, early_second, grad_ssm_next = tie(
        (one, back_block, early_first, early_second, grad_ssm_two[1])
    )
    back_block = scatter_block(back_block, factors, coords, inward[:-1])
    early_block = scatter_second(early_first, early_second, factors, coords)
    two = scan_pull_two(grad_ssm_next)
    two, back_block, early_block = tie((two, back_block, early_block))
    back_sum = scatter_block(back_block, factors, coords, inward[-1:])
    early_sum = scatter_block(early_block, factors, coords, inward)
    back_sum = back_sum.reshape(rows, -1)
    early_sum = early_sum.reshape(rows, -1)
    (
        grad_x,
        grad_step,
        grad_bc,
        grad_conv,
        grad_conv_bias,
        grad_conv_bc,
        grad_conv_bc_bias,
        grad_decay,
        grad_step_bias,
    ) = inputs_pull(
        (
            grad_xc + jnp.concatenate([one[0], two[0]], 1),
            one[1] + two[1],
            jnp.concatenate([one[2], two[2]], 1),
            jnp.concatenate([one[3], two[3]], 1),
        )
    )
    normed_early = dot(grad_early, early_w, ((1,), (1,)))
    grad_late = jnp.concatenate(
        [
            grad_x.astype(BF16),
            grad_step.astype(BF16),
            jnp.zeros((n_rows, step_cols - n_heads), BF16),
            grad_bc.astype(BF16),
        ],
        1,
    )
    grad_late, early_sum, back_sum, normed_early = tie(
        (grad_late, early_sum, back_sum, normed_early)
    )
    late_full = dot(normed, grad_late, ((0,), (0,))).astype(BF16)
    late_cols = inner + step_cols
    late_half = grad_late.shape[1] // 256 * 128
    late_first, late_second = scatter_first(
        late_full[:, :late_half], late_full[:, late_half:], factors, coords
    )
    late_block = scatter_second(late_first, late_second, factors, coords)
    late_sum = scatter_block(late_block, factors, coords, inward).reshape(rows, -1)
    early_sum, back_sum, late_sum = [v.astype(F32) for v in (early_sum, back_sum, late_sum)]
    grad_normed = normed_early + dot(grad_late[:, :late_cols], late_w, ((1,), (1,)))
    grad_normed = grad_normed + dot(grad_late[:, late_cols:], state_w, ((1,), (1,)))
    grad_normed = split_tensor(grad_normed, part)
    grad_gain_first = jnp.sum(grad_normed * unit_first, 0)
    inputs_grad = grad_middle + norm_back(grad_normed, unit_first, inv_first, gain_first)

    small_grads = (
        grad_gain_first,
        grad_gain_second,
        widen(grad_conv, 1),
        widen(grad_conv_bias, 0),
        widen(grad_gain_mix, 0),
        grad_conv_bc,
        grad_conv_bc_bias,
    )
    columns = []
    for item, grad in zip(small_parts, small_grads):
        if item.ndim == 2:
            piece = grad.reshape(item.shape[0], n_dp * n_parts, -1).transpose(1, 0, 2)
        else:
            piece = grad
        columns.append(piece.reshape(n_dp * n_parts, -1))
    piece_rows = jnp.concatenate(columns, 1).reshape(n_dp, n_parts * n_small)
    heads = jnp.concatenate([grad_decay, grad_step_bias, grad_skip])
    filled = n_parts * n_small + heads.shape[0]
    lines = -(-filled // 1024) * 8
    packed = jnp.concatenate(
        [
            piece_rows,
            jnp.broadcast_to(heads[None, :], (n_dp, heads.shape[0])),
            jnp.zeros((n_dp, lines * 128 - filled), F32),
        ],
        1,
    ).reshape(tuple(factors) + (lines, 128))
    for axis in range(len(factors)):
        packed = reduce_axis(packed, factors, coords, axis)
    packed = packed.reshape(-1)
    pair = packed[: n_parts * n_small].reshape(n_parts, n_small)
    mine = lax.dynamic_index_in_dim(pair, part, 0, keepdims=False) + swap(
        lax.dynamic_index_in_dim(pair, 1 - part, 0, keepdims=False)
    )
    small_out = []
    at = 0
    for item in small_parts:
        small_out.append(mine[at : at + item.size].reshape(item.shape))
        at += item.size
    head_sums = packed[n_parts * n_small : filled].reshape(3, n_heads)

    state_sum = late_sum[:, late_cols:]
    half = rows // n_parts
    state_grad = lax.dynamic_slice_in_dim(state_sum, part * half, half, 0) + swap(
        lax.dynamic_slice_in_dim(state_sum, (1 - part) * half, half, 0)
    )
    mix_grad = jnp.concatenate(
        [
            early_sum[:, :inner].reshape(rows, n_heads, head_dim),
            late_sum[:, :inner].reshape(rows, n_heads, head_dim),
        ],
        -1,
    )
    return (
        output,
        inputs_grad,
        small_out[0],
        mix_grad,
        late_sum[:, inner : inner + n_heads],
        state_grad,
        small_out[2],
        small_out[3],
        small_out[5],
        small_out[6],
        head_sums[0],
        head_sums[1],
        head_sums[2],
        small_out[4],
        early_sum[:, inner:].reshape(attn_in.shape),
        back_sum[:, 3 * hid : 3 * hid + inner].T.reshape(mixer_out.shape),
        back_sum[:, 3 * hid + inner :].T.reshape(attn_out.shape),
        small_out[1],
        back_sum[:, : 2 * hid].reshape(ffn_in.shape),
        back_sum[:, 2 * hid : 3 * hid].T,
    )


def solution(mesh):
    return jax.shard_map(
        per_device,
        mesh=mesh,
        in_specs=(
            P(("dp", "tensor"), None),
            P("dp"),
            P(("dp", "tensor"), None),
            P(("dp", "tensor")),
            P("dp", "tensor", None),
            P("dp", "tensor"),
            P(("dp", "tensor"), None),
            P(None, ("dp", "tensor")),
            P(("dp", "tensor")),
            P(None, ("dp", "tensor")),
            P(("dp", "tensor")),
            P("tensor"),
            P("tensor"),
            P("tensor"),
            P(("dp", "tensor")),
            P("dp", "tensor", None),
            P("tensor", None, "dp"),
            P("tensor", None, "dp"),
            P(("dp", "tensor")),
            P("dp", None, "tensor"),
            P("tensor", "dp"),
        ),
        out_specs=(
            P(("dp", "tensor"), None),
            P(("dp", "tensor"), None),
            P(("dp", "tensor")),
            P("dp", "tensor", None),
            P("dp", "tensor"),
            P(("dp", "tensor"), None),
            P(None, ("dp", "tensor")),
            P(("dp", "tensor")),
            P(None, ("dp", "tensor")),
            P(("dp", "tensor")),
            P("tensor"),
            P("tensor"),
            P("tensor"),
            P(("dp", "tensor")),
            P("dp", "tensor", None),
            P("tensor", None, "dp"),
            P("tensor", None, "dp"),
            P(("dp", "tensor")),
            P("dp", None, "tensor"),
            P("tensor", "dp"),
        ),
        check_vma=False,
    )
```

```python
import jax
import jax.numpy as jnp
from jax import lax
from jax.sharding import PartitionSpec as P

QPK = 4
ADIM = 64
NGH = 12
BLK = 256
QBLK = 512

PREC = lax.Precision.DEFAULT
EXACT = lax.Precision.HIGHEST
EPS = 1e-05
ROPE_BASE = 100000000000.0
F32 = jnp.float32
BF16 = jnp.bfloat16


def grid_of(size):
    factors = []
    while size > 1:
        factors.append(2)
        size //= 2
    return tuple(factors)


def coordinates(index, factors):
    coords = []
    for size in reversed(factors):
        coords.append(index % size)
        index = index // size
    return coords[::-1]


def exchange(value, factors, axis):
    stride = 2 ** (len(factors) - 1 - axis)
    pairs = [(index, index ^ stride) for index in range(2 ** len(factors))]
    return lax.ppermute(value, "dp", pairs)


def gather_axis(block, factors, coords, axis):
    other = exchange(block, factors, axis)
    return lax.dynamic_slice_in_dim(
        jnp.concatenate([other, block, other], axis), 1 - coords[axis], 2, axis
    )


def gather_block(block, factors, coords, axes):
    for axis in axes:
        block = gather_axis(block, factors, coords, axis)
    return block


def gather_first(block, factors, coords, cut):
    n_axes = len(factors)
    first, second = block[..., :cut], block[..., cut:]
    first = gather_axis(first, factors, coords, n_axes - 2)
    second = gather_axis(second, factors, coords, n_axes - 1)
    return first, second


def gather_second(first, second, factors, coords):
    n_axes = len(factors)
    first = gather_axis(first, factors, coords, n_axes - 1)
    second = gather_axis(second, factors, coords, n_axes - 2)
    return first.reshape(-1, first.shape[-1]), second.reshape(-1, second.shape[-1])


def reduce_axis(blocks, factors, coords, axis):
    def pick(place):
        return lax.dynamic_slice_in_dim(blocks, place, 1, axis)

    got = exchange(pick(1 - coords[axis]), factors, axis)
    return (pick(coords[axis]).astype(F32) + got.astype(F32)).astype(blocks.dtype)


def scatter_first(first, second, factors, coords):
    n_axes = len(factors)
    rows = first.shape[0] // 2**n_axes
    first = first.reshape(tuple(factors) + (rows, first.shape[1]))
    second = second.reshape(tuple(factors) + (rows, second.shape[1]))
    first = reduce_axis(first, factors, coords, n_axes - 1)
    second = reduce_axis(second, factors, coords, n_axes - 2)
    return first, second


def scatter_second(first, second, factors, coords):
    n_axes = len(factors)
    first = reduce_axis(first, factors, coords, n_axes - 2)
    second = reduce_axis(second, factors, coords, n_axes - 1)
    return jnp.concatenate([first, second], n_axes + 1)


def scatter_block(block, factors, coords, axes):
    for axis in axes:
        block = reduce_axis(block, factors, coords, axis)
    return block


def tie(values):
    return lax.optimization_barrier(values)


def swap(value):
    return lax.ppermute(value, "tensor", [(0, 1), (1, 0)])


def join_tensor(mine, part, axis=0):
    other = swap(mine)
    return lax.dynamic_slice_in_dim(
        jnp.concatenate([other, mine, other], axis),
        (1 - part) * mine.shape[axis],
        2 * mine.shape[axis],
        axis,
    )


def split_tensor(value, part):
    half = value.shape[0] // 2
    give = lax.dynamic_slice_in_dim(value, (1 - part) * half, half, 0).astype(BF16)
    keep = lax.dynamic_slice_in_dim(value, part * half, half, 0).astype(F32)
    return keep + swap(give).astype(F32)


def rotate(values, cosine, sine):
    half_dim = values.shape[-1] // 2
    bshape = (values.shape[0],) + (1,) * (values.ndim - 2) + (half_dim,)
    cosine = cosine.reshape(bshape)
    sine = sine.reshape(bshape)
    first_half = values[..., :half_dim]
    second_half = values[..., half_dim:]
    return jnp.concatenate(
        [first_half * cosine - second_half * sine, second_half * cosine + first_half * sine], -1
    )


def seg_conv(values, taps, shift_bias, same_doc):
    n_rows = values.shape[0]
    n_taps = taps.shape[0]
    padded = jnp.pad(values, ((n_taps - 1, 0), (0, 0)))
    result = shift_bias[None, :] + taps[n_taps - 1][None, :] * values
    for offset in range(n_taps - 1):
        result = (
            result
            + taps[offset][None, :] * padded[offset : offset + n_rows] * same_doc[offset][:, None]
        )
    return result


def ssd_scan(inner, steps, decays, b_state, c_state, segment, block_len):
    n_rows, n_heads, head_dim = inner.shape
    n_blocks = n_rows // block_len
    x_blk = inner.reshape(n_blocks, block_len, n_heads, head_dim).transpose(0, 2, 1, 3)
    dt_blk = steps.reshape(n_blocks, block_len, n_heads).transpose(0, 2, 1)
    within = jnp.arange(block_len, dtype=jnp.int32)
    causal = within[:, None] >= within[None, :]
    cumul = jnp.einsum(
        "ts,csh->cht",
        causal.astype(F32),
        decays.reshape(n_blocks, block_len, n_heads),
        precision=EXACT,
    )
    b_blk = b_state.reshape(n_blocks, block_len, -1)
    c_blk = c_state.reshape(n_blocks, block_len, -1)
    seg_blk = segment.reshape(n_blocks, block_len)
    allowed = (seg_blk[:, :, None] == seg_blk[:, None, :]) & causal[None]
    differ = cumul[:, :, :, None] - cumul[:, :, None, :]
    kernel = jnp.exp(jnp.where(allowed[:, None], differ, -1e30))
    inner_prod = jnp.einsum("ctn,csn->cts", c_blk, b_blk, precision=PREC)
    x_step = x_blk * dt_blk[..., None]
    weights_ts = inner_prod[:, None] * kernel
    y_inner = jnp.einsum("chts,chsp->chtp", weights_ts, x_step, precision=PREC)
    last_seg = seg_blk[:, -1]
    to_end = (
        jnp.exp(cumul[:, :, -1:] - cumul)
        * (seg_blk == last_seg[:, None]).astype(F32)[:, None, :]
    )
    local_state = jnp.einsum(
        "chsp,csn->chpn", x_step * to_end[..., None], b_blk, precision=PREC
    )
    prev_seg = jnp.concatenate([jnp.full((1,), -1, dtype=jnp.int32), last_seg[:-1]])
    carry_keep = jnp.exp(cumul[:, :, -1]) * (last_seg == prev_seg).astype(F32)[:, None]
    state = jnp.zeros(local_state.shape[1:], F32)
    entering = [state]
    for block in range(n_blocks - 1):
        state = state * carry_keep[block][:, None, None] + local_state[block]
        entering.append(state)
    entering = jnp.stack(entering)
    from_start = jnp.exp(cumul) * (seg_blk == prev_seg[:, None]).astype(F32)[:, None, :]
    y_state = jnp.einsum("ctn,chpn->chtp", c_blk, entering, precision=PREC)
    total = y_inner + y_state * from_start[..., None]
    return total.transpose(0, 2, 1, 3).reshape(n_rows, n_heads * head_dim)


def mamba_inputs(
    proj_x, proj_step, proj_bc, conv_w, conv_b, conv_s, conv_sb, log_decay, bias_step, same_doc
):
    x_conv = jax.nn.silu(seg_conv(proj_x, conv_w, conv_b, same_doc))
    bc_conv = jax.nn.silu(seg_conv(proj_bc, conv_s, conv_sb, same_doc))
    steps = jax.nn.softplus(proj_step + bias_step[None, :])
    decays = -steps * jnp.exp(log_decay)[None, :]
    return x_conv, bc_conv, steps, decays


def mamba_scan(x_conv, bc_conv, steps, decays, segment):
    n_rows, n_heads = steps.shape
    n_state = bc_conv.shape[1] // 2
    return ssd_scan(
        x_conv.reshape(n_rows, n_heads, -1),
        steps,
        decays,
        bc_conv[:, :n_state],
        bc_conv[:, n_state:],
        segment,
        BLK,
    )


def mamba_gate(ssm, x_conv, gate_z, gain_skip, gain_mix):
    n_channels = gate_z.shape[1]
    head_dim = n_channels // gain_skip.shape[0]
    ssm = ssm + jnp.repeat(gain_skip, head_dim)[None, :] * x_conv
    gated = ssm * jax.nn.silu(gate_z)
    width = NGH * head_dim
    normed = []
    for first in range(0, n_channels, width):
        group = gated[:, first : first + width]
        normed.append(group * lax.rsqrt(jnp.mean(group * group, -1, keepdims=True) + EPS))
    return jnp.concatenate(normed, 1) * gain_mix[None, :]


def masked_scores(q_blk, keys, allowed, scaling):
    scores = jnp.einsum("tqd,sd->qts", q_blk, keys, preferred_element_type=F32) * scaling
    return jnp.where(allowed[None], scores, -1e30)


def query_blocks(segment):
    n_rows = segment.shape[0]
    q_len = min(QBLK, n_rows)
    index = jnp.arange(n_rows, dtype=jnp.int32)
    blocks = []
    for start in range(0, n_rows, q_len):
        stop = start + q_len
        allowed = (segment[start:stop, None] == segment[None, :stop]) & (
            index[start:stop, None] >= index[None, :stop]
        )
        blocks.append((start, stop, allowed))
    return blocks


def attend_forward(queries, keys, vals, blocks, scaling):
    outs, norms = [], []
    for start, stop, allowed in blocks:
        scores = masked_scores(queries[start:stop], keys[:stop], allowed, scaling)
        topmost = jnp.max(scores, -1, keepdims=True)
        expo = jnp.exp(scores - topmost)
        total = jnp.sum(expo, -1, keepdims=True)
        probs = (expo / total).astype(BF16)
        outs.append(jnp.einsum("qts,sd->tqd", probs, vals[:stop], preferred_element_type=F32))
        norms.append(topmost + jnp.log(total))
    return jnp.concatenate(outs, 0), norms


def attend_backward(queries, keys, vals, blocks, norms, grad_out, scaling):
    grad_q = []
    grad_keys = jnp.zeros(keys.shape, F32)
    grad_vals = jnp.zeros(vals.shape, F32)
    for (start, stop, allowed), norm in zip(blocks, norms):
        q_blk, dout = queries[start:stop], grad_out[start:stop]
        scores = masked_scores(q_blk, keys[:stop], allowed, scaling)
        probs = jnp.exp(scores - norm)
        dv = jnp.einsum("qts,tqd->sd", probs.astype(BF16), dout, preferred_element_type=F32)
        dprobs = jnp.einsum("tqd,sd->qts", dout, vals[:stop], preferred_element_type=F32)
        dscores = probs * (dprobs - jnp.sum(probs * dprobs, -1, keepdims=True))
        low = dscores.astype(BF16)
        grad_q.append(
            jnp.einsum("qts,sd->tqd", low, keys[:stop], preferred_element_type=F32) * scaling
        )
        dk = jnp.einsum("qts,tqd->sd", low, q_blk, preferred_element_type=F32) * scaling
        tail = ((0, keys.shape[0] - stop), (0, 0))
        grad_keys = grad_keys + jnp.pad(dk, tail)
        grad_vals = grad_vals + jnp.pad(dv, tail)
    return jnp.concatenate(grad_q, 0), grad_keys, grad_vals


def norm_back(grad_normed, unit_rows, inv_scale, gain):
    scaled = grad_normed * gain[None, :]
    return inv_scale * (scaled - unit_rows * jnp.mean(scaled * unit_rows, -1, keepdims=True))


def dot(a, b, dims):
    return lax.dot_general(a, b, (dims, ((), ())), preferred_element_type=F32)


def per_device(
    inputs,
    segments,
    cotangent,
    norm_gain,
    mix_in,
    step_in,
    state_in,
    conv_inner,
    conv_inner_bias,
    conv_state,
    conv_state_bias,
    decay_log,
    step_bias,
    skip_gain,
    mixer_gain,
    attn_in,
    mixer_out,
    attn_out,
    ffn_gain,
    ffn_in,
    ffn_down,
):
    part = lax.axis_index("tensor")
    place = lax.axis_index("dp")
    n_dp = lax.axis_size("dp")
    n_parts = lax.axis_size("tensor")
    factors = grid_of(n_dp)
    coords = coordinates(place, factors)
    rows = mix_in.shape[0]
    n_heads, twice = mix_in.shape[1:]
    head_dim = twice // 2
    inner = n_heads * head_dim
    n_rows = segments.shape[0]
    qkv_cols = attn_in.shape[1] * attn_in.shape[2]
    state_cols = state_in.shape[1]
    hid = ffn_down.shape[0]
    attn_cols = attn_out.shape[0] * attn_out.shape[1]
    d_model = inputs.shape[1]

    small_parts = (
        norm_gain,
        ffn_gain,
        conv_inner,
        conv_inner_bias,
        mixer_gain,
        conv_state,
        conv_state_bias,
    )
    small = jnp.concatenate([a.reshape(-1) for a in small_parts] + [state_in.reshape(-1)])
    n_small = small.shape[0] - state_in.size
    both = join_tensor(small.reshape(1, -1), part)
    state_rows = both[:, n_small:].reshape(rows, state_cols)
    small_cols = -(-n_parts * n_small // rows)
    small_block = jnp.pad(
        both[:, :n_small].reshape(-1), (0, rows * small_cols - n_parts * n_small)
    ).reshape(rows, small_cols)
    step_cols = -(-n_heads // 128) * 128
    pad_cols = -(-small_cols // 128) * 128
    side = jnp.concatenate(
        [state_rows, jnp.pad(small_block, ((0, 0), (0, pad_cols - small_cols)))], 1
    )
    front = jnp.concatenate(
        [
            mix_in[..., :head_dim].reshape(rows, inner),
            attn_in.reshape(rows, qkv_cols),
            mix_in[..., head_dim:].reshape(rows, inner),
            jnp.pad(step_in, ((0, 0), (0, step_cols - n_heads))),
        ],
        1,
    )
    back = jnp.concatenate(
        [
            mixer_out.reshape(inner, rows).T,
            attn_out.reshape(attn_cols, rows).T,
            ffn_down.T,
            ffn_in.reshape(rows, 2 * hid),
        ],
        1,
    )
    early_cols = inner + qkv_cols
    n_axes = len(factors)
    outer = range(n_axes - 2)
    inward = range(n_axes - 3, -1, -1)

    def as_block(shard):
        return shard.reshape((1,) * n_axes + shard.shape)

    front_block = gather_block(as_block(front), factors, coords, outer)
    early_w, late_w = gather_second(
        *gather_first(front_block, factors, coords, early_cols), factors, coords
    )
    side_w = gather_block(as_block(side), factors, coords, range(n_axes))
    side_w = side_w.reshape(-1, side.shape[1])
    early_w, late_w, side_w, back = tie((early_w, late_w, side_w, back))
    out_cols = inner + attn_cols
    state_w = side_w[:, :state_cols]

    smalls = side_w.reshape(n_dp, rows, -1)[:, :, state_cols : state_cols + small_cols]
    smalls = smalls.reshape(n_dp, -1)[:, : n_parts * n_small].reshape(n_dp * n_parts, n_small)
    smalls = smalls.astype(F32)
    pieces = []
    at = 0
    for item in small_parts:
        piece = smalls[:, at : at + item.size].reshape((-1,) + item.shape)
        at += item.size
        if item.ndim == 2:
            piece = piece.transpose(1, 0, 2).reshape(item.shape[0], -1)
        else:
            piece = piece.reshape(-1)
        pieces.append(piece)
    gain_first, gain_second, conv_full, conv_bias_full, gain_mix_full, conv_bc, conv_bc_bias = pieces

    def local_cols(array, axis_dim):
        return lax.dynamic_slice_in_dim(array, part * inner, inner, axis_dim)

    def widen(local, axis_dim):
        full_shape = list(local.shape)
        full_shape[axis_dim] = inner * n_parts
        return lax.dynamic_update_slice_in_dim(
            jnp.zeros(full_shape, F32), local, part * inner, axis_dim
        )

    conv_local = local_cols(conv_full, 1)
    conv_bias_local = local_cols(conv_bias_full, 0)
    gain_mixer = local_cols(gain_mix_full, 0)

    cot_full = join_tensor(cotangent, part)
    inputs_f = inputs.astype(F32)
    inv_first = lax.rsqrt(jnp.mean(inputs_f * inputs_f, -1, keepdims=True) + EPS)
    unit_first = inputs_f * inv_first
    normed = join_tensor((unit_first * gain_first[None, :]).astype(BF16), part)

    row_index = jnp.arange(n_rows, dtype=jnp.int32)
    places = place * n_rows + row_index - segments
    half_dim = ADIM // 2
    freqs = ROPE_BASE ** (-2.0 * jnp.arange(half_dim, dtype=F32) / ADIM)
    angles = places.astype(F32)[:, None] * freqs[None, :]
    cosine, sine = jnp.cos(angles), jnp.sin(angles)
    n_taps = conv_inner.shape[0]
    same_doc = [(places >= n_taps - 1 - k).astype(F32) for k in range(n_taps - 1)]

    proj_early = dot(normed, early_w, ((1,), (0,)))
    proj_late = dot(normed, late_w, ((1,), (0,)))
    proj_bc = dot(normed, state_w, ((1,), (0,)))

    back_block = gather_block(as_block(back), factors, coords, outer[:1])

    def inputs_of(*values):
        return mamba_inputs(*values, same_doc)

    def scan_of(*values):
        return mamba_scan(*values, segments)

    (x_conv, bc_conv, steps, decays), inputs_pull = jax.vjp(
        inputs_of,
        proj_late[:, :inner],
        proj_late[:, inner : inner + n_heads],
        proj_bc,
        conv_local,
        conv_bias_local,
        conv_bc,
        conv_bc_bias,
        decay_log,
        step_bias,
    )
    scaling = ADIM ** (-0.5)
    q_cols = QPK * ADIM
    q_part = proj_early[:, inner : inner + q_cols].reshape(n_rows, QPK, ADIM)
    k_part = proj_early[:, inner + q_cols : inner + q_cols + ADIM]
    queries = rotate(q_part, cosine, sine).astype(BF16)
    keys = rotate(k_part, cosine, sine).astype(BF16)
    vals = proj_early[:, inner + q_cols + ADIM :].astype(BF16)
    blocks = query_blocks(segments)
    queries, back_block = tie((queries, back_block))
    back_block = gather_block(back_block, factors, coords, outer[1:])
    attended, norms = attend_forward(queries, keys, vals, blocks, scaling)
    attended_low = attended.reshape(n_rows, attn_cols).astype(BF16)
    back_block, x_conv, attended_low = tie((back_block, x_conv, attended_low))
    half_heads = n_heads // 2
    half_inner = inner // 2

    def halves_of(value, size):
        return value[:, :size], value[:, size:]

    x_two = halves_of(x_conv, half_inner)
    step_two = halves_of(steps, half_heads)
    decay_two = halves_of(decays, half_heads)
    back_first, back_second = gather_first(back_block, factors, coords, out_cols + hid)
    ssm_one, scan_pull_one = jax.vjp(scan_of, x_two[0], bc_conv, step_two[0], decay_two[0])
    back_first, back_second, ssm_one, x_next = tie((back_first, back_second, ssm_one, x_two[1]))
    outs_w, ffin_full = tie(gather_second(back_first, back_second, factors, coords))
    mixout_t = outs_w[:, :inner]
    attnout_t = outs_w[:, inner:out_cols]
    out_t = outs_w[:, :out_cols]
    down_t = outs_w[:, out_cols:]
    ssm_two, scan_pull_two = jax.vjp(scan_of, x_next, bc_conv, step_two[1], decay_two[1])
    mamba_value, gate_pull = jax.vjp(
        mamba_gate,
        jnp.concatenate([ssm_one, ssm_two], 1),
        x_conv,
        proj_early[:, :inner],
        skip_gain,
        gain_mixer,
    )
    mamba_low = mamba_value.astype(BF16)
    mix_low = jnp.concatenate([mamba_low, attended_low], 1)
    mixed = split_tensor(dot(mix_low, out_t, ((1,), (1,))), part)
    middle = inputs_f + mixed
    inv_second = lax.rsqrt(jnp.mean(middle * middle, -1, keepdims=True) + EPS)
    unit_second = middle * inv_second
    hidden = join_tensor((unit_second * gain_second[None, :]).astype(BF16), part)
    gate_up = dot(hidden, ffin_full, ((1,), (0,)))
    gate = gate_up[:, :hid]
    upper = gate_up[:, hid:]
    sigma = jax.nn.sigmoid(gate)
    active = (gate * sigma * upper).astype(BF16)
    ffn_value = split_tensor(dot(active, down_t, ((1,), (1,))), part)
    output = (middle + ffn_value).astype(BF16)

    grad_down = dot(cot_full, active, ((0,), (0,)))
    grad_active = dot(cot_full, down_t, ((1,), (0,)))
    grad_gate = grad_active * upper * sigma * (1.0 + gate * (1.0 - sigma))
    grad_up = grad_active * gate * sigma
    grad_gu = jnp.concatenate([grad_gate.astype(BF16), grad_up.astype(BF16)], 1)
    grad_ffin = dot(hidden, grad_gu, ((0,), (0,)))
    grad_hidden = split_tensor(dot(grad_gu, ffin_full, ((1,), (1,))), part)
    grad_gain_second = jnp.sum(grad_hidden * unit_second, 0)
    grad_middle = cotangent.astype(F32) + norm_back(
        grad_hidden, unit_second, inv_second, gain_second
    )
    grad_mixed = join_tensor(grad_middle.astype(BF16), part)
    grad_outs = dot(grad_mixed, mix_low, ((0,), (0,)))
    back_first, back_second = scatter_first(
        grad_ffin.astype(BF16),
        jnp.concatenate([grad_down.astype(BF16), grad_outs.astype(BF16)], 1),
        factors,
        coords,
    )
    grad_att = dot(grad_mixed, attnout_t, ((1,), (0,))).astype(BF16)
    grad_mamba = dot(grad_mixed, mixout_t, ((1,), (0,)))
    grad_q, grad_k, grad_v = attend_backward(
        queries, keys, vals, blocks, norms, grad_att.reshape(n_rows, QPK, ADIM), scaling
    )
    grad_q = rotate(grad_q, cosine, -sine).reshape(n_rows, q_cols)
    grad_k = rotate(grad_k, cosine, -sine)
    grad_ssm, grad_xc, grad_z, grad_skip, grad_gain_mix = gate_pull(grad_mamba)
    grad_early = jnp.concatenate(
        [
            grad_z.astype(BF16),
            grad_q.astype(BF16),
            grad_k.astype(BF16),
            grad_v.astype(BF16),
        ],
        1,
    )
    early_full = dot(normed, grad_early, ((0,), (0,))).astype(BF16)
    early_half = early_cols // 256 * 128
    early_full, back_first, back_second, grad_ssm = tie(
        (early_full, back_first, back_second, grad_ssm)
    )
    back_block = scatter_second(back_first, back_second, factors, coords)
    early_first, early_second = scatter_first(
        early_full[:, :early_half], early_full[:, early_half:], factors, coords
    )
    grad_ssm_two = halves_of(grad_ssm, half_inner)
    one = scan_pull_one(grad_ssm_two[0])
    one, back_block, early_first, early_second, grad_ssm_next = tie(
        (one, back_block, early_first, early_second, grad_ssm_two[1])
    )
    back_block = scatter_block(back_block, factors, coords, inward[:-1])
    early_block = scatter_second(early_first, early_second, factors, coords)
    two = scan_pull_two(grad_ssm_next)
    two, back_block, early_block = tie((two, back_block, early_block))
    back_sum = scatter_block(back_block, factors, coords, inward[-1:])
    early_sum = scatter_block(early_block, factors, coords, inward)
    back_sum = back_sum.reshape(rows, -1)
    early_sum = early_sum.reshape(rows, -1)
    (
        grad_x,
        grad_step,
        grad_bc,
        grad_conv,
        grad_conv_bias,
        grad_conv_bc,
        grad_conv_bc_bias,
        grad_decay,
        grad_step_bias,
    ) = inputs_pull(
        (
            grad_xc + jnp.concatenate([one[0], two[0]], 1),
            one[1] + two[1],
            jnp.concatenate([one[2], two[2]], 1),
            jnp.concatenate([one[3], two[3]], 1),
        )
    )
    normed_early = dot(grad_early, early_w, ((1,), (1,)))
    grad_late = jnp.concatenate(
        [
            grad_x.astype(BF16),
            grad_step.astype(BF16),
            jnp.zeros((n_rows, step_cols - n_heads), BF16),
            grad_bc.astype(BF16),
        ],
        1,
    )
    grad_late, early_sum, back_sum, normed_early = tie(
        (grad_late, early_sum, back_sum, normed_early)
    )
    late_full = dot(normed, grad_late, ((0,), (0,))).astype(BF16)
    late_cols = inner + step_cols
    late_half = grad_late.shape[1] // 256 * 128
    late_first, late_second = scatter_first(
        late_full[:, :late_half], late_full[:, late_half:], factors, coords
    )
    late_block = scatter_second(late_first, late_second, factors, coords)
    late_sum = scatter_block(late_block, factors, coords, inward).reshape(rows, -1)
    early_sum, back_sum, late_sum = [v.astype(F32) for v in (early_sum, back_sum, late_sum)]
    grad_normed = normed_early + dot(grad_late[:, :late_cols], late_w, ((1,), (1,)))
    grad_normed = grad_normed + dot(grad_late[:, late_cols:], state_w, ((1,), (1,)))
    grad_normed = split_tensor(grad_normed, part)
    grad_gain_first = jnp.sum(grad_normed * unit_first, 0)
    inputs_grad = grad_middle + norm_back(grad_normed, unit_first, inv_first, gain_first)

    small_grads = (
        grad_gain_first,
        grad_gain_second,
        widen(grad_conv, 1),
        widen(grad_conv_bias, 0),
        widen(grad_gain_mix, 0),
        grad_conv_bc,
        grad_conv_bc_bias,
    )
    columns = []
    for item, grad in zip(small_parts, small_grads):
        if item.ndim == 2:
            piece = grad.reshape(item.shape[0], n_dp * n_parts, -1).transpose(1, 0, 2)
        else:
            piece = grad
        columns.append(piece.reshape(n_dp * n_parts, -1))
    piece_rows = jnp.concatenate(columns, 1).reshape(n_dp, n_parts * n_small)
    heads = jnp.concatenate([grad_decay, grad_step_bias, grad_skip])
    filled = n_parts * n_small + heads.shape[0]
    lines = -(-filled // 1024) * 8
    packed = jnp.concatenate(
        [
            piece_rows,
            jnp.broadcast_to(heads[None, :], (n_dp, heads.shape[0])),
            jnp.zeros((n_dp, lines * 128 - filled), F32),
        ],
        1,
    ).reshape(tuple(factors) + (lines, 128))
    for axis in range(len(factors)):
        packed = reduce_axis(packed, factors, coords, axis)
    packed = packed.reshape(-1)
    pair = packed[: n_parts * n_small].reshape(n_parts, n_small)
    mine = lax.dynamic_index_in_dim(pair, part, 0, keepdims=False) + swap(
        lax.dynamic_index_in_dim(pair, 1 - part, 0, keepdims=False)
    )
    small_out = []
    at = 0
    for item in small_parts:
        small_out.append(mine[at : at + item.size].reshape(item.shape))
        at += item.size
    head_sums = packed[n_parts * n_small : filled].reshape(3, n_heads)

    state_sum = late_sum[:, late_cols:]
    half = rows // n_parts
    state_grad = lax.dynamic_slice_in_dim(state_sum, part * half, half, 0) + swap(
        lax.dynamic_slice_in_dim(state_sum, (1 - part) * half, half, 0)
    )
    mix_grad = jnp.concatenate(
        [
            early_sum[:, :inner].reshape(rows, n_heads, head_dim),
            late_sum[:, :inner].reshape(rows, n_heads, head_dim),
        ],
        -1,
    )
    return (
        output,
        inputs_grad,
        small_out[0],
        mix_grad,
        late_sum[:, inner : inner + n_heads],
        state_grad,
        small_out[2],
        small_out[3],
        small_out[5],
        small_out[6],
        head_sums[0],
        head_sums[1],
        head_sums[2],
        small_out[4],
        early_sum[:, inner:].reshape(attn_in.shape),
        back_sum[:, 3 * hid : 3 * hid + inner].T.reshape(mixer_out.shape),
        back_sum[:, 3 * hid + inner :].T.reshape(attn_out.shape),
        small_out[1],
        back_sum[:, : 2 * hid].reshape(ffn_in.shape),
        back_sum[:, 2 * hid : 3 * hid].T,
    )


def solution(mesh):
    return jax.shard_map(
        per_device,
        mesh=mesh,
        in_specs=(
            P(("dp", "tensor"), None),
            P("dp"),
            P(("dp", "tensor"), None),
            P(("dp", "tensor")),
            P("dp", "tensor", None),
            P("dp", "tensor"),
            P(("dp", "tensor"), None),
            P(None, ("dp", "tensor")),
            P(("dp", "tensor")),
            P(None, ("dp", "tensor")),
            P(("dp", "tensor")),
            P("tensor"),
            P("tensor"),
            P("tensor"),
            P(("dp", "tensor")),
            P("dp", "tensor", None),
            P("tensor", None, "dp"),
            P("tensor", None, "dp"),
            P(("dp", "tensor")),
            P("dp", None, "tensor"),
            P("tensor", "dp"),
        ),
        out_specs=(
            P(("dp", "tensor"), None),
            P(("dp", "tensor"), None),
            P(("dp", "tensor")),
            P("dp", "tensor", None),
            P("dp", "tensor"),
            P(("dp", "tensor"), None),
            P(None, ("dp", "tensor")),
            P(("dp", "tensor")),
            P(None, ("dp", "tensor")),
            P(("dp", "tensor")),
            P("tensor"),
            P("tensor"),
            P("tensor"),
            P(("dp", "tensor")),
            P("dp", "tensor", None),
            P("tensor", None, "dp"),
            P("tensor", None, "dp"),
            P(("dp", "tensor")),
            P("dp", None, "tensor"),
            P("tensor", "dp"),
        ),
        check_vma=False,
    )
```
